32 devices in a mesh: grp: 2 (over y), res: 4 (over z), br: 2 (over core), aux: 2 (over x).
Axes of the slice: x: 2, y: 2, z: 4, core: 2. Of those that a mesh axis runs over, the one named last changes fastest.
Arguments:
- homolog_features: bfloat16 [32, 128, 256], P(('grp', 'br', 'aux'), 'res'), parts along dimension 0, may hold values from -6 to 6
- couple_features: bfloat16 [256, 128, 128], P(('grp', 'res'), ('br', 'aux')), parts along dimension 0, may hold values from -6 to 6
- symbol_ids: int32 [32, 128], P(('grp', 'br', 'aux'), 'res'), parts along dimension 0, may hold values from 0 to 22
- entry_present: int32 [32, 128], P(('grp', 'br', 'aux'), 'res'), parts along dimension 0, may hold values 0 or 1
- amino_present: int32 [256], P('grp'), parts along dimension 0, may hold values 0 or 1
- symbol_lookup_matrix: bfloat16 [23, 256], replicated, may hold values from -3 to 3
- horizontal_entry_matrix: bfloat16 [256, 1024], replicated, may hold values from -0.375 to 0.375
- couple_logit_matrix: bfloat16 [128, 8], replicated, may hold values from -40 to 40, as said below
- horizontal_exit_matrix: bfloat16 [256, 256], replicated, may hold values from -0.375 to 0.375
- vertical_entry_matrix: bfloat16 [256, 1024], replicated, may hold values from -0.375 to 0.375
- vertical_exit_matrix: bfloat16 [256, 256], replicated, may hold values from -0.375 to 0.375
- feedforward_first_matrix: bfloat16 [256, 1024], replicated, may hold values from -0.375 to 0.375
- feedforward_second_matrix: bfloat16 [1024, 256], replicated, may hold values from -0.1875 to 0.1875
- trimul_entry_matrix: bfloat16 [128, 640], replicated, may hold values from -0.5 to 0.5
- trimul_exit_matrix: bfloat16 [128, 128], replicated, may hold values from -0.5 to 0.5
Outputs:
- alignment_output: bfloat16 [32, 128, 256], P(('grp', 'br', 'aux'), 'res'), parts along dimension 0
- pair_output: bfloat16 [256, 128, 128], P(('grp', 'res'), ('br', 'aux')), parts along dimension 0
The draws below stay inside these ranges and needn't reach their ends.
There are 2 independent parts, one for each index of `grp`. The reference program is written for one: setup_inputs(seed, part) draws one part's arguments, and reference() takes and returns one part's arrays. A program takes and returns all parts, laid end to end along the dimension named above; an argument that names none is the same for every part. Nothing has to cross between parts.
Inputs may be any that keep to these rules, and one draw needn't show every extreme that they name: `couple_logit_matrix`: a projection of the 128 pair channels onto the 8 heads.
All inputs are finite; a program needn't handle non-finite values. No bound on the sum of `entry_present` on one device may be relied on, other than what follows from the above.
Results may differ from the reference program's by a relative error of at most 0.008.
Values may be sent and summed in bfloat16 or wider, within the bound.
No kernel may reach another device: no remote copies, remote signals or barrier semaphores. Data moves between devices by JAX's collectives and lax.ppermute only.
A program may use at most 64 MiB of HBM per device.

```python
import jax
import jax.numpy as jnp
from jax import lax

FEATURE_DEPTH = 256
CZ = 128
FOCI_TOTAL = 8
ATTEND_SPAN = 32
SYMBOL_KINDS = 23
HOMOLOG_TOTAL = 16
AMINO_TOTAL = 128
WIDENED_LAYER = 1024


def draw_couple_logit_matrix(key, part):
    base = jax.random.normal(jax.random.fold_in(key, 11), (CZ, FOCI_TOTAL), jnp.float32) * CZ ** (-0.5)
    return base.astype(jnp.bfloat16)


def plant(values, key, low, top_value):
    shape = values.shape
    spot = [jax.random.randint(jax.random.fold_in(key, axis), (), 0, shape[axis]) for axis in range(len(shape))]
    values = values.at[tuple(spot)].set(low)
    longest = shape.index(max(shape))
    spot[longest] = (spot[longest] + 1) % shape[longest]
    return values.at[tuple(spot)].set(top_value)


def level_of(own_key, dims, split, least, largest):
    def one(dim, parts):
        draws = jax.random.uniform(jax.random.fold_in(jax.random.fold_in(own_key, 6), dim), (parts,), jnp.float32, least / len(split), largest / len(split))
        return jnp.repeat(jnp.exp(draws), dims[dim] // parts).reshape((-1,) + (1,) * (len(dims) - dim - 1))

    level = one(*split[0])
    for cut in split[1:]:
        level = level * one(*cut)
    return level


def gaussian(key, extent, spread, reach, pieces=(), kind=jnp.bfloat16):
    array = jax.random.normal(key, extent, jnp.float32) * spread
    if len(pieces) > 0:
        array = level_of(key, extent, pieces, -0.22, 0.18) * array
    return jnp.clip(array, min=-reach, max=reach).astype(kind)


def setup_inputs(seed: int = 0, part: int = 0) -> dict:
    key_list = jax.random.split(jax.random.key(seed), 16)
    own_keys = jax.random.split(jax.random.fold_in(key_list[15], part), 16)
    homolog_features = gaussian(own_keys[0], (HOMOLOG_TOTAL, AMINO_TOTAL, FEATURE_DEPTH), 1.0, 6.0, ((0, 4), (1, 4)))
    couple_features = gaussian(own_keys[1], (AMINO_TOTAL, AMINO_TOTAL, CZ), 1.0, 6.0, ((0, 4), (1, 4)))
    symbol_ids = plant(jax.random.randint(own_keys[2], (HOMOLOG_TOTAL, AMINO_TOTAL), 0, SYMBOL_KINDS), jax.random.fold_in(own_keys[2], 1), 0, SYMBOL_KINDS - 1).astype(jnp.int32)
    entry_present = plant((jax.random.randint(own_keys[3], (HOMOLOG_TOTAL, AMINO_TOTAL), 0, 4) < 3).astype(jnp.int32), jax.random.fold_in(own_keys[3], 1), 0, 1)
    amino_present = plant((jax.random.randint(own_keys[4], (AMINO_TOTAL,), 0, 8) < 7).astype(jnp.int32), jax.random.fold_in(own_keys[4], 1), 0, 1)
    symbol_lookup_matrix = gaussian(key_list[5], (SYMBOL_KINDS, FEATURE_DEPTH), 0.5, 3.0)
    horizontal_entry_matrix = gaussian(key_list[6], (FEATURE_DEPTH, 4 * FEATURE_DEPTH), FEATURE_DEPTH ** -0.5, 0.375)
    couple_logit_matrix = draw_couple_logit_matrix(jax.random.fold_in(key_list[15], 71), part)
    horizontal_exit_matrix = gaussian(key_list[8], (FEATURE_DEPTH, FEATURE_DEPTH), FEATURE_DEPTH ** -0.5, 0.375)
    vertical_entry_matrix = gaussian(key_list[9], (FEATURE_DEPTH, 4 * FEATURE_DEPTH), FEATURE_DEPTH ** -0.5, 0.375)
    vertical_exit_matrix = gaussian(key_list[10], (FEATURE_DEPTH, FEATURE_DEPTH), FEATURE_DEPTH ** -0.5, 0.375)
    feedforward_first_matrix = gaussian(key_list[11], (FEATURE_DEPTH, WIDENED_LAYER), FEATURE_DEPTH ** -0.5, 0.375)
    feedforward_second_matrix = gaussian(key_list[12], (WIDENED_LAYER, FEATURE_DEPTH), WIDENED_LAYER ** -0.5, 0.1875)
    trimul_entry_matrix = gaussian(key_list[13], (CZ, 5 * CZ), CZ ** -0.5, 0.5)
    trimul_exit_matrix = gaussian(key_list[14], (CZ, CZ), CZ ** -0.5, 0.5)
    return dict(homolog_features=homolog_features, couple_features=couple_features, symbol_ids=symbol_ids, entry_present=entry_present, amino_present=amino_present, symbol_lookup_matrix=symbol_lookup_matrix, horizontal_entry_matrix=horizontal_entry_matrix, couple_logit_matrix=couple_logit_matrix, horizontal_exit_matrix=horizontal_exit_matrix, vertical_entry_matrix=vertical_entry_matrix, vertical_exit_matrix=vertical_exit_matrix, feedforward_first_matrix=feedforward_first_matrix, feedforward_second_matrix=feedforward_second_matrix, trimul_entry_matrix=trimul_entry_matrix, trimul_exit_matrix=trimul_exit_matrix)


epsilon = 1e-05
masked_fill_value = 1000000000.0

def normalize(inputs):
    values = inputs.astype(jnp.float32)
    average = lax.optimization_barrier(jnp.mean(values, axis=-1, keepdims=True))
    centred = values - average
    variance = lax.optimization_barrier(jnp.mean(centred * centred, axis=-1, keepdims=True))
    return centred * lax.rsqrt(variance + epsilon)

def apply_projection(row_block, weight):
    flattened = row_block.reshape(-1, row_block.shape[-1])
    result = jnp.dot(flattened, weight, preferred_element_type=jnp.float32)
    return result.reshape(row_block.shape[:-1] + (weight.shape[1],))

def attend(queries, key_rows, value_rows, bias_block, penalty):
    scores = jnp.einsum('qhd,khd->hqk', queries.astype(jnp.float32), key_rows.astype(jnp.float32)) * ATTEND_SPAN ** (-0.5)
    scores = scores + bias_block + penalty
    row_max = lax.optimization_barrier(jnp.max(scores, axis=-1, keepdims=True))
    powers = jnp.exp(scores - row_max)
    weights = (powers / lax.optimization_barrier(jnp.sum(powers, axis=-1, keepdims=True))).astype(jnp.bfloat16)
    return jnp.einsum('hqk,khd->qhd', weights.astype(jnp.float32), value_rows.astype(jnp.float32))

def reference(homolog_features, couple_features, symbol_ids, entry_present, amino_present, symbol_lookup_matrix, horizontal_entry_matrix, couple_logit_matrix, horizontal_exit_matrix, vertical_entry_matrix, vertical_exit_matrix, feedforward_first_matrix, feedforward_second_matrix, trimul_entry_matrix, trimul_exit_matrix):
    indicator_symbols = (symbol_ids[..., None] == jnp.arange(SYMBOL_KINDS, dtype=jnp.int32)[None, None, :]).astype(jnp.float32)
    symbol_vectors = homolog_features.astype(jnp.float32) + jnp.einsum('zas,sv->zav', indicator_symbols, symbol_lookup_matrix.astype(jnp.float32))
    normed_first = normalize(symbol_vectors).astype(jnp.bfloat16)
    horizontal_combined = apply_projection(normed_first, horizontal_entry_matrix)
    horizontal_queries = horizontal_combined[..., :FEATURE_DEPTH].astype(jnp.bfloat16).reshape(HOMOLOG_TOTAL, AMINO_TOTAL, FOCI_TOTAL, ATTEND_SPAN)
    horizontal_keyset = horizontal_combined[..., FEATURE_DEPTH:2 * FEATURE_DEPTH].astype(jnp.bfloat16).reshape(HOMOLOG_TOTAL, AMINO_TOTAL, FOCI_TOTAL, ATTEND_SPAN)
    horizontal_payload = horizontal_combined[..., 2 * FEATURE_DEPTH:3 * FEATURE_DEPTH].astype(jnp.bfloat16).reshape(HOMOLOG_TOTAL, AMINO_TOTAL, FOCI_TOTAL, ATTEND_SPAN)
    horizontal_sigmoid = jax.nn.sigmoid(horizontal_combined[..., 3 * FEATURE_DEPTH:])
    pair_norm = normalize(couple_features).astype(jnp.bfloat16)
    pair_bias = apply_projection(pair_norm, couple_logit_matrix).transpose(2, 0, 1)
    key_mask_penalty = masked_fill_value * (entry_present.astype(jnp.float32) - 1.0)

    def one_row(items):
        queries, key_rows, value_rows, penalty = items
        return attend(queries, key_rows, value_rows, pair_bias, penalty[None, None, :])
    horizontal_context = lax.map(one_row, (horizontal_queries, horizontal_keyset, horizontal_payload, key_mask_penalty))
    horizontal_result = (horizontal_sigmoid * horizontal_context.reshape(HOMOLOG_TOTAL, AMINO_TOTAL, FEATURE_DEPTH)).astype(jnp.bfloat16)
    after_row = symbol_vectors + apply_projection(horizontal_result, horizontal_exit_matrix)
    normed_second = normalize(after_row).astype(jnp.bfloat16)
    vertical_combined = apply_projection(normed_second, vertical_entry_matrix)
    vertical_queries = vertical_combined[..., :FEATURE_DEPTH].astype(jnp.bfloat16).reshape(HOMOLOG_TOTAL, AMINO_TOTAL, FOCI_TOTAL, ATTEND_SPAN)
    vertical_keyset = vertical_combined[..., FEATURE_DEPTH:2 * FEATURE_DEPTH].astype(jnp.bfloat16).reshape(HOMOLOG_TOTAL, AMINO_TOTAL, FOCI_TOTAL, ATTEND_SPAN)
    vertical_payload = vertical_combined[..., 2 * FEATURE_DEPTH:3 * FEATURE_DEPTH].astype(jnp.bfloat16).reshape(HOMOLOG_TOTAL, AMINO_TOTAL, FOCI_TOTAL, ATTEND_SPAN)
    vertical_sigmoid = jax.nn.sigmoid(vertical_combined[..., 3 * FEATURE_DEPTH:])

    def one_column(items):
        queries, key_rows, value_rows, penalty = items
        return attend(queries, key_rows, value_rows, jnp.zeros((1, 1, 1), jnp.float32), penalty[None, None, :])
    vertical_context = lax.map(one_column, (vertical_queries.transpose(1, 0, 2, 3), vertical_keyset.transpose(1, 0, 2, 3), vertical_payload.transpose(1, 0, 2, 3), key_mask_penalty.T))
    vertical_result = (vertical_sigmoid * vertical_context.transpose(1, 0, 2, 3).reshape(HOMOLOG_TOTAL, AMINO_TOTAL, FEATURE_DEPTH)).astype(jnp.bfloat16)
    after_column_update = after_row + apply_projection(vertical_result, vertical_exit_matrix)
    normed_third = normalize(after_column_update).astype(jnp.bfloat16)
    hidden_units = jax.nn.relu(apply_projection(normed_third, feedforward_first_matrix)).astype(jnp.bfloat16)
    alignment_output = (after_column_update + apply_projection(hidden_units, feedforward_second_matrix)).astype(jnp.bfloat16)
    tri_all = apply_projection(pair_norm, trimul_entry_matrix)
    valid_res = amino_present.astype(jnp.float32)
    pair_valid = (valid_res[:, None] * valid_res[None, :])[..., None]
    left_side = (jax.nn.sigmoid(tri_all[..., CZ:2 * CZ]) * tri_all[..., :CZ] * pair_valid).astype(jnp.bfloat16)
    right_side = (jax.nn.sigmoid(tri_all[..., 3 * CZ:4 * CZ]) * tri_all[..., 2 * CZ:3 * CZ] * pair_valid).astype(jnp.bfloat16)
    out_gate = jax.nn.sigmoid(tri_all[..., 4 * CZ:])
    product = jnp.einsum('kic,kjc->ijc', left_side.astype(jnp.float32), right_side.astype(jnp.float32)).astype(jnp.bfloat16)
    normed_final = normalize(product).astype(jnp.bfloat16)
    pair_output = (couple_features.astype(jnp.float32) + out_gate * apply_projection(normed_final, trimul_exit_matrix)).astype(jnp.bfloat16)
    return (alignment_output, pair_output)
```

```python
import functools

import jax
import jax.numpy as jnp
from jax import lax
from jax.experimental import pallas as pl
from jax.experimental.pallas import tpu as pltpu
from jax.sharding import PartitionSpec as P

epsilon = 1e-05
masked_fill_value = 1000000000.0
bf16 = jnp.bfloat16
f32 = jnp.float32
SIDE = ("br", "aux")
ALL = ("res", "br", "aux")
NT = (((1,), (1,)), ((), ()))
TN = (((0,), (0,)), ((), ()))


def normalize(values):
    average = jnp.mean(values, axis=-1, keepdims=True)
    centred = values - average
    variance = jnp.mean(centred * centred, axis=-1, keepdims=True)
    return centred * lax.rsqrt(variance + epsilon)


def sigmoid(values):
    return 1.0 / (1.0 + jnp.exp(-values))


def dot(left, right):
    return jnp.dot(left, right, preferred_element_type=f32)


def iota(shape, dim):
    return lax.broadcasted_iota(jnp.int32, shape, dim)


def round_up(count, step):
    return -(-count // step) * step


def side_index():
    return lax.axis_index("br") * lax.axis_size("aux") + lax.axis_index("aux")


def embed_kernel(features, ids, present, table, embedded, payload, tail):
    lines, positions, depth = features.shape
    kinds = table.shape[0]
    rows = lines * positions
    for line in range(lines):
        onehot = (iota((kinds, positions), 0) == ids[line : line + 1, :]).astype(bf16)
        token = lax.dot_general(onehot, table[...], TN, preferred_element_type=f32)
        values = features[line].astype(f32) + token
        span = slice(line * positions, (line + 1) * positions)
        embedded[span, :] = values
        payload[span, :] = normalize(values).astype(bf16)
    tail[...] = jnp.zeros_like(tail)
    tail[:lines, :positions] = present[...].astype(f32)
    payload[rows:, :] = tail[...].astype(bf16)


def attend(queries, keys, values, bias, heads):
    count, depth = queries.shape
    width = depth // heads
    own = (iota((heads, depth), 1) // width == iota((heads, depth), 0)).astype(f32)
    spread = (queries[:, None, :] * own[None]).reshape(count * heads, depth).astype(bf16)
    scores = lax.dot_general(spread, keys, NT, preferred_element_type=f32) * width ** (-0.5)
    scores = bias(scores)
    powers = jnp.exp(scores - jnp.max(scores, axis=-1, keepdims=True))
    weights = (powers * (1.0 / jnp.sum(powers, axis=-1, keepdims=True))).astype(bf16)
    mixed = dot(weights, values).reshape(count, heads, depth)
    return jnp.sum(mixed * own[None], axis=1)


def row_kernel(relative, side_relative, sides, lines, positions, *refs):
    terms, refs = refs[:sides], refs[sides:]
    blocks = refs[: len(refs) - 10]
    own, embedded, entry, leave, after, payload, bias, keys, values, mix = refs[len(refs) - 10 :]
    depth = leave.shape[0]
    heads = bias.shape[0] // positions
    rows = lines * positions
    key_count = bias.shape[1]
    me = lax.axis_index("res")
    lanes = terms[0].shape[1]
    per = lanes // positions
    side = side_index()
    sums = []
    for term in terms:
        held = positions * heads // per
        base = term.shape[0] - 3 * held
        sums.append(
            term[base : base + held, :].astype(f32)
            + term[base + held : base + 2 * held, :].astype(f32)
            + term[base + 2 * held :, :].astype(f32)
        )
    place = iota((heads, key_count), 1) // positions
    for line in range(positions):
        total = jnp.zeros((heads, key_count), f32)
        for slot, values_of in enumerate(sums):
            source = (side ^ slot) if side_relative else slot
            part = values_of[(line // per) * heads : (line // per + 1) * heads]
            part = pltpu.roll(part, ((source - line % per + lanes) % per) * positions, 1)
            part = jnp.concatenate([part] * (key_count // lanes), axis=1)
            total = jnp.where(place == source, part, total)
        bias[line * heads : (line + 1) * heads, :] = total
    penalty = jnp.zeros((payload.shape[0] - rows, key_count), f32)
    for slot, block in enumerate(blocks):
        source = (me ^ slot) if relative else slot
        block = rows_of(block, payload.shape[0], depth)
        place = iota((depth, key_count), 0)
        place = (place < positions) & (iota((depth, key_count), 1) == place + source * positions)
        penalty += dot(block[rows:, :], place.astype(bf16))
        projected = dot(block[:rows, :], entry[:, depth : 3 * depth]).astype(bf16)
        for line in range(lines):
            span = pl.ds(pl.multiple_of(source * positions, positions), positions)
            part = projected[line * positions : (line + 1) * positions]
            keys[line, span, :] = part[:, :depth]
            values[line, span, :] = part[:, depth:]
    penalty = masked_fill_value * (penalty - 1.0)
    normed = own[:rows, :]
    queries = dot(normed, entry[:, :depth]).astype(bf16).astype(f32)
    gate = sigmoid(dot(normed, entry[:, 3 * depth :]))
    for line in range(lines):
        span = slice(line * positions, (line + 1) * positions)
        fixed = lambda scores, line=line: scores + bias[...] + penalty[line : line + 1, :]
        mixed = attend(queries[span], keys[line], values[line], fixed, heads)
        mix[span, :] = (gate[span] * mixed).astype(bf16)
    result = embedded[...] + dot(mix[...], leave[...])
    after[...] = result
    payload[:rows, :] = normalize(result).astype(bf16)
    payload[rows:, :] = own[rows:, :]


def column_kernel(lines, positions, group, heads, *refs):
    blocks = refs[: len(refs) - 10]
    own, after, entry, leave, first, second, output, keys, values, mix = refs[len(refs) - 10 :]
    depth = leave.shape[0]
    rows = lines * positions
    presence = []
    for slot, block in enumerate(blocks):
        projected = dot(block[:rows, :], entry[:, depth : 3 * depth])
        span = slice(slot * lines, (slot + 1) * lines)
        keys[span] = projected[:, :depth].reshape(lines, positions, depth)
        values[span] = projected[:, depth:].reshape(lines, positions, depth)
        presence.append(block[rows:, :])
    tail = presence[0].shape[0]
    presence = jnp.concatenate(presence, axis=0)
    normed = own[:rows, :]
    queries = dot(normed, entry[:, :depth]).astype(bf16).astype(f32)
    queries = queries.reshape(lines, positions, depth)
    gate = sigmoid(dot(normed, entry[:, 3 * depth :])).reshape(lines, positions, depth)
    key_count = len(blocks) * lines * group
    row = iota((presence.shape[0], key_count), 0)
    lane = iota((presence.shape[0], key_count), 1)
    chosen = (row % tail < lines) & ((row // tail) * lines + row % tail == lane // group)
    shape = (lines * group * heads, key_count)
    same = (iota(shape, 0) // heads) % group == iota(shape, 1) % group
    for start in range(0, positions, group):
        span = slice(start, start + group)
        pick = (iota((depth, key_count), 0) == start + iota((depth, key_count), 1) % group)
        held = dot(presence, pick.astype(bf16))
        held = jnp.sum(jnp.where(chosen, held, 0.0), axis=0, keepdims=True)
        penalty = masked_fill_value * (held - 1.0)
        fixed = lambda scores: jnp.where(same, scores + penalty, -jnp.inf)
        mixed = attend(
            queries[:, span].reshape(lines * group, depth),
            keys[:, span].reshape(key_count, depth).astype(bf16),
            values[:, span].reshape(key_count, depth).astype(bf16),
            fixed,
            heads,
        )
        mix[:, span] = gate[:, span] * mixed.reshape(lines, group, depth)
    mixed = mix[...].reshape(rows, depth).astype(bf16)
    result = after[...] + dot(mixed, leave[...])
    hidden = jnp.maximum(dot(normalize(result).astype(bf16), first[...]), 0.0).astype(bf16)
    result = result + dot(hidden, second[...])
    output[...] = result.astype(bf16).reshape(output.shape)


def fetch(sources, buffers, semaphores):
    copies = [
        pltpu.make_async_copy(source, buffer, semaphores.at[index])
        for index, (source, buffer) in enumerate(zip(sources, buffers))
    ]
    for copy in copies:
        copy.start()
    for copy in copies:
        copy.wait()


def split(values):
    high = values.astype(bf16)
    rest = values - high.astype(f32)
    middle = rest.astype(bf16)
    return high, middle, (rest - middle.astype(f32)).astype(bf16)


def start_kernel(count, present, *refs):
    sources, outputs, rest = refs[:count], refs[count : count + 6], refs[count + 6 :]
    buffers, semaphores, tail = rest[:count], rest[count], rest[count + 1]
    fetch(sources, buffers, semaphores)
    embedded, payload, bundle, gate, terms, near = outputs
    embed_kernel(*buffers[:4], embedded, payload, tail)
    present_row, pairs, entry, logits = buffers[4:]
    lines, positions, width = pairs.shape
    heads = logits.shape[0]
    normed = normalize(pairs[...].astype(f32).reshape(lines * positions, width)).astype(bf16)
    logit = lax.dot_general(logits[...], normed, NT, preferred_element_type=f32)
    held = terms.shape[0] // 3
    for index, term in enumerate(split(logit)):
        for part in range(held // heads):
            base = index * held + part * heads
            terms[base : base + heads, :] = term[:, part * width : (part + 1) * width]
    projected = dot(normed, entry[:, 2 * width :])
    gate[...] = sigmoid(projected[:, 2 * width :])
    operand = (sigmoid(projected[:, width : 2 * width]) * projected[:, :width]).astype(bf16)
    mask_right(lax.axis_index("res"), operand, present, present_row, near)
    base = lines * positions
    bundle[:base, :] = pairs[...].reshape(base, width)
    for part in range(payload.shape[1] // width):
        span = slice(base + part * payload.shape[0], base + (part + 1) * payload.shape[0])
        bundle[span, :] = payload[:, part * width : (part + 1) * width]


def rows_of(block, count, depth):
    if block.shape == (count, depth):
        return block[...]
    parts = depth // block.shape[1]
    base = block.shape[0] - parts * count
    return jnp.concatenate(
        [block[base + part * count : base + (part + 1) * count, :] for part in range(parts)], axis=1
    )


def turn_kernel(pairs, entry, terms, out):
    width = pairs.shape[2]
    operand = gated(pairs, entry[:, : 2 * width])
    out[: operand.shape[0], :] = operand
    out[operand.shape[0] :, :] = terms[...]


def gated(pairs, weight):
    lines, positions, width = pairs.shape
    normed = normalize(pairs[...].astype(f32).reshape(lines * positions, width)).astype(bf16)
    projected = dot(normed, weight)
    return (sigmoid(projected[:, width:]) * projected[:, :width]).astype(bf16)


def left_kernel(pairs, entry, left):
    width = pairs.shape[2]
    left[...] = gated(pairs, entry[:, : 2 * width])


def mask_right(source, operand, present, present_row, right):
    lines, positions, width = right.shape
    lane = iota((positions, present_row.shape[1]), 1)
    lane = lane == iota((positions, present_row.shape[1]), 0) + side_index() * positions
    valid = jnp.where(lane, present_row[...].astype(f32), 0.0)
    valid = jnp.sum(valid, axis=1, keepdims=True)
    operand = operand.astype(f32)
    for line in range(lines):
        both = valid * present[source * lines + line].astype(f32)
        right[line] = (operand[line * positions : (line + 1) * positions] * both).astype(
            right.dtype
        )


def right_operand(relative, slot, present, present_row, pairs, entry, right):
    width = pairs.shape[2]
    source = (lax.axis_index("res") ^ slot) if relative else slot
    operand = gated(pairs, entry[:, 2 * width : 4 * width])
    mask_right(source, operand, present, present_row, right)


def pick_left(relative, slot, lefts, left):
    source = (lax.axis_index("res") ^ slot) if relative[0] else slot
    side = side_index()
    for place, block in enumerate(lefts):
        held = (side ^ place) if relative[1] else place

        @pl.when(held == source)
        def _():
            left[...] = block[...].astype(f32).reshape(left.shape)


def accumulate(left, right, total_in, total):
    step = 4
    depth, positions, width = right.shape

    def body(index, carry):
        base = index * step
        sums = [None if total_in is None else total_in[base + t] for t in range(step)]
        for line in range(depth):
            line_right = right[line].astype(f32)
            for t in range(step):
                term = left[line, pl.ds(base + t, 1), :] * line_right
                sums[t] = term if sums[t] is None else sums[t] + term
        for t in range(step):
            total[base + t] = sums[t]
        return carry

    lax.fori_loop(0, total.shape[0] // step, body, 0)


def middle_kernel(relative, slots, *refs):
    rights, lefts = refs[: len(slots)], refs[len(slots) : -2]
    total, left = refs[-2:]
    for index, slot in enumerate(slots):
        pick_left(relative, slot, lefts, left)
        accumulate(left, rights[index], total if index else None, total)


def last_kernel(relative, slot, *refs):
    present, present_row, pairs, entry, total_in, own, gate, leave = refs[:8]
    lefts, (out, left, right, total) = refs[8:-4], refs[-4:]
    lines, positions, width = out.shape
    pick_left(relative, slot, lefts, left)
    right_operand(relative[0], slot, present, present_row, pairs, entry, right)
    accumulate(left, right, total_in, total)
    me = lax.axis_index("res")
    for line in range(lines):
        total[line] = total[line] * present[me * lines + line].astype(f32)
    product = total[...].reshape(lines * positions, width).astype(bf16).astype(f32)
    update = gate[...] * dot(normalize(product).astype(bf16), leave[...])
    out[...] = (own[...].astype(f32) + update.reshape(out.shape)).astype(bf16)


def far_kernel(lines, present, present_row, bundle, entry, right):
    width = bundle.shape[1]
    pairs = bundle[: lines * right.shape[1], :].reshape(right.shape)
    operand = gated(pairs, entry[:, 2 * width : 4 * width])
    mask_right(lax.axis_index("res") ^ 1, operand, present, present_row, right)


def partial_kernel(other_half, own, beside, other, other_beside, near, far, total, left):
    half = lax.axis_index("res") // 2
    wanted = (1 - half) if other_half else half
    mine = lax.axis_index("br") == wanted
    straight = lax.axis_index("res") % 2 == lax.axis_index("aux")
    count = total.shape[0]
    lines = near.shape[0]

    def load(first, second):
        for slot, block in enumerate((first, second)):
            for line in range(lines):
                base = line * count
                left[slot * lines + line] = block[base : base + count, :].astype(f32)

    other_core = jnp.logical_not(mine)
    crossed = jnp.logical_not(straight)
    pl.when(mine & straight)(lambda: load(own, beside))
    pl.when(mine & crossed)(lambda: load(beside, own))
    pl.when(other_core & straight)(lambda: load(other, other_beside))
    pl.when(other_core & crossed)(lambda: load(other_beside, other))
    step = 8

    def body(index, carry):
        base = index * step
        sums = [None] * step
        for line in range(2 * lines):
            right = near[line] if line < lines else far[line - lines]
            for t in range(step):
                term = left[line, pl.ds(base + t, 1), :] * right
                sums[t] = term if sums[t] is None else sums[t] + term
        for t in range(step):
            total[base + t] = sums[t].astype(total.dtype)
        return carry

    lax.fori_loop(0, count // step, body, 0)


def finish_kernel(present, kept, own, gate, leave, *refs):
    received, (out, total) = refs[:-2], refs[-2:]
    lines, positions, width = out.shape
    me = lax.axis_index("res")
    each = lines // len(received)
    for line in range(lines):
        sums = kept[line] + received[line // each][line % each].astype(f32)
        total[line] = sums * present[me * lines + line].astype(f32)
    product = total[...].reshape(lines * positions, width).astype(bf16).astype(f32)
    update = gate[...] * dot(normalize(product).astype(bf16), leave[...])
    out[...] = (own[...].astype(f32) + update.reshape(out.shape)).astype(bf16)


def gather(block, axis):
    size = lax.axis_size(axis)
    if size in (1, 2, 4):
        return [block] + [flip(block, axis, d) for d in range(1, size)], True
    whole = lax.all_gather(block, axis)
    return [whole[i] for i in range(size)], False


def flip(block, axis, bit=1):
    return lax.ppermute(block, axis, [(i, i ^ bit) for i in range(lax.axis_size(axis))])


def gather_side(block, ahead=()):
    if lax.axis_size("br") == 2 and lax.axis_size("aux") == 2:
        near = flip(block, "br")
        far = flip(block, "aux")
        far = lax.optimization_barrier((far, *ahead))[0]
        return [block, far, near, flip(far, "br")], True
    whole = lax.all_gather(block, SIDE)
    return [whole[i] for i in range(whole.shape[0])], False


def shape(dims, kind):
    return jax.ShapeDtypeStruct(dims, kind)


def call(kernel, out_shape, scratch=(), smem=0, after=(), hbm=False):
    def run(*args):
        count, unread = len(args), len(after)

        def ordered(*refs):
            kernel(*refs[:count], *refs[count + unread :])

        return pl.pallas_call(
            ordered,
            out_shape=out_shape,
            in_specs=[pl.BlockSpec(memory_space=pltpu.SMEM)] * smem
            + [pl.BlockSpec(memory_space=pltpu.HBM if hbm else pltpu.VMEM)] * (count - smem)
            + [pl.BlockSpec(memory_space=pl.ANY)] * unread,
            out_specs=jax.tree.map(lambda _: pl.BlockSpec(memory_space=pltpu.VMEM), out_shape),
            scratch_shapes=list(scratch),
            compiler_params=pltpu.CompilerParams(vmem_limit_bytes=(62 if hbm else 48) * 1024 * 1024),
            cost_estimate=pl.CostEstimate(flops=1, bytes_accessed=1, transcendentals=0),
        )(*args, *after)

    return run


def triangle_by_gather(pairs, presence, entry, leave, gate):
    res = lax.axis_size("res")
    side = lax.axis_size("br") * lax.axis_size("aux")
    rows, cols, width = pairs.shape
    cube = pltpu.VMEM((rows, cols, width), f32)
    turned = lax.ppermute(
        pairs, ALL, [(r * side + b, b * side + r) for r in range(res) for b in range(side)]
    )
    left = call(left_kernel, shape((rows * cols, width), bf16))(turned, entry)
    lefts, left_relative = gather_side(left)
    blocks, pair_relative = gather(pairs, "res")
    relative = (pair_relative, left_relative)
    slots = list(range(res - 1))
    rights = [
        call(
            functools.partial(right_operand, pair_relative, slot), shape(pairs.shape, bf16), smem=1
        )(*presence, blocks[slot], entry)
        for slot in slots
    ]
    total = call(
        functools.partial(middle_kernel, relative, slots), shape(pairs.shape, f32), [cube]
    )(*rights, *lefts)
    return call(
        functools.partial(last_kernel, relative, res - 1),
        shape(pairs.shape, bf16),
        [cube, cube, cube],
        smem=1,
    )(*presence, blocks[-1], entry, total, pairs, gate, leave, *lefts)


def turn_pairs(pairs):
    index = lambda half, low, br, aux: ((half * 2 + low) * 2 + br) * 2 + aux
    every = [(h, low, br, aux) for h in (0, 1) for low in (0, 1) for br in (0, 1) for aux in (0, 1)]
    return lax.ppermute(
        pairs, ALL, [(index(h, l, br, a), index(h, a, br, l)) for h, l, br, a in every]
    )


def on_device(
    homolog_features,
    couple_features,
    symbol_ids,
    entry_present,
    amino_present,
    symbol_lookup_matrix,
    horizontal_entry_matrix,
    couple_logit_matrix,
    horizontal_exit_matrix,
    vertical_entry_matrix,
    vertical_exit_matrix,
    feedforward_first_matrix,
    feedforward_second_matrix,
    trimul_entry_matrix,
    trimul_exit_matrix,
):
    lines, positions, depth = homolog_features.shape
    pair_rows, pair_cols, width = couple_features.shape
    heads = couple_logit_matrix.shape[1]
    res = lax.axis_size("res")
    side = lax.axis_size("br") * lax.axis_size("aux")
    rows = lines * positions
    tail = round_up(lines, 16)
    residues = positions * res
    area = pair_rows * pair_cols
    held = pair_rows * pair_cols * heads // width
    presence = [amino_present, amino_present[None, :]]
    halves = (res, lax.axis_size("br"), lax.axis_size("aux")) == (4, 2, 2)

    args = (
        homolog_features,
        symbol_ids,
        entry_present,
        symbol_lookup_matrix,
        amino_present[None, :],
        couple_features,
        trimul_entry_matrix,
        couple_logit_matrix.T,
    )
    embedded, payload, bundle, gate, terms, near = call(
        functools.partial(start_kernel, len(args)),
        (
            shape((rows, depth), f32),
            shape((rows + tail, depth), bf16),
            shape((area + (rows + tail) * (depth // width), width), bf16),
            shape((area, width), f32),
            shape((3 * held, width), bf16),
            shape(couple_features.shape, f32),
        ),
        [pltpu.VMEM(x.shape, x.dtype) for x in args]
        + [pltpu.SemaphoreType.DMA((len(args),)), pltpu.VMEM((tail, depth), f32)],
        smem=1,
        hbm=True,
    )(amino_present, *args)
    pending = ()
    if halves:
        beside = flip(bundle, "res")
        row_blocks = [payload, beside, flip(payload, "res", 2), flip(payload, "res", 3)]
        row_relative = True
        turned = call(turn_kernel, shape((area + 3 * held, width), bf16))(
            turn_pairs(couple_features), trimul_entry_matrix, terms
        )
        terms, side_relative = gather_side(turned, (beside, *row_blocks[2:]))
        far = call(
            functools.partial(far_kernel, pair_rows),
            shape(couple_features.shape, f32),
            smem=1,
            after=(turned,),
        )(*presence, beside, trimul_entry_matrix)

        def sums(other_half, kind, after):
            return call(
                functools.partial(partial_kernel, other_half),
                shape(couple_features.shape, kind),
                [pltpu.VMEM((2 * pair_rows, pair_cols, width), f32)],
                after=after,
            )(*terms, near, far)

        sent = sums(True, bf16, ())
        received = flip(sent, "res", 2)
        pending = (sent,)
    else:
        row_blocks, row_relative = gather(payload, "res")
        terms, side_relative = gather_side(terms)

    after, payload = call(
        functools.partial(row_kernel, row_relative, side_relative, side, lines, positions),
        (shape((rows, depth), f32), shape((rows + tail, depth), bf16)),
        [
            pltpu.VMEM((pair_rows * heads, residues), f32),
            pltpu.VMEM((lines, residues, depth), bf16),
            pltpu.VMEM((lines, residues, depth), bf16),
            pltpu.VMEM((rows, depth), bf16),
        ],
        after=pending,
    )(*terms, *row_blocks, payload, embedded, horizontal_entry_matrix, horizontal_exit_matrix)
    column_blocks, _ = gather_side(payload)
    if halves:
        kept = sums(False, f32, (payload,))
        pending = (kept,)
    group = 8
    alignment_output = call(
        functools.partial(column_kernel, lines, positions, group, heads),
        shape((lines, positions, depth), bf16),
        [
            pltpu.VMEM((side * lines, positions, depth), f32),
            pltpu.VMEM((side * lines, positions, depth), f32),
            pltpu.VMEM((lines, positions, depth), f32),
        ],
        after=pending,
    )(
        *column_blocks,
        payload,
        after,
        vertical_entry_matrix,
        vertical_exit_matrix,
        feedforward_first_matrix,
        feedforward_second_matrix,
    )
    if halves:
        pair_output = call(
            finish_kernel,
            shape(couple_features.shape, bf16),
            [pltpu.VMEM(couple_features.shape, f32)],
            smem=1,
        )(amino_present, kept, couple_features, gate, trimul_exit_matrix, received)
    else:
        pair_output = triangle_by_gather(
            couple_features, presence, trimul_entry_matrix, trimul_exit_matrix, gate
        )
    return (alignment_output, pair_output)


def solution(mesh):
    return jax.shard_map(
        on_device,
        mesh=mesh,
        in_specs=(
            P(("grp", "br", "aux"), "res", None),
            P(("grp", "res"), ("br", "aux"), None),
            P(("grp", "br", "aux"), "res"),
            P(("grp", "br", "aux"), "res"),
            P("grp"),
            P(),
            P(),
            P(),
            P(),
            P(),
            P(),
            P(),
            P(),
            P(),
            P(),
        ),
        out_specs=(P(("grp", "br", "aux"), "res", None), P(("grp", "res"), ("br", "aux"), None)),
        check_vma=False,
    )
```

```python
import functools

import jax
import jax.numpy as jnp
from jax import lax
from jax.experimental import pallas as pl
from jax.experimental.pallas import tpu as pltpu
from jax.sharding import PartitionSpec as P

epsilon = 1e-05
masked_fill_value = 1000000000.0
bf16 = jnp.bfloat16
f32 = jnp.float32
SIDE = ("br", "aux")
ALL = ("res", "br", "aux")
NT = (((1,), (1,)), ((), ()))
TN = (((0,), (0,)), ((), ()))


def normalize(values):
    average = jnp.mean(values, axis=-1, keepdims=True)
    centred = values - average
    variance = jnp.mean(centred * centred, axis=-1, keepdims=True)
    return centred * lax.rsqrt(variance + epsilon)


def sigmoid(values):
    return 1.0 / (1.0 + jnp.exp(-values))


def dot(left, right):
    return jnp.dot(left, right, preferred_element_type=f32)


def iota(shape, dim):
    return lax.broadcasted_iota(jnp.int32, shape, dim)


def round_up(count, step):
    return -(-count // step) * step


def side_index():
    return lax.axis_index("br") * lax.axis_size("aux") + lax.axis_index("aux")


def embed_kernel(features, ids, present, table, embedded, payload, tail):
    lines, positions, depth = features.shape
    kinds = table.shape[0]
    rows = lines * positions
    for line in range(lines):
        onehot = (iota((kinds, positions), 0) == ids[line : line + 1, :]).astype(bf16)
        token = lax.dot_general(onehot, table[...], TN, preferred_element_type=f32)
        values = features[line].astype(f32) + token
        span = slice(line * positions, (line + 1) * positions)
        embedded[span, :] = values
        payload[span, :] = normalize(values).astype(bf16)
    tail[...] = jnp.zeros_like(tail)
    tail[:lines, :positions] = present[...].astype(f32)
    payload[rows:, :] = tail[...].astype(bf16)


def attend(queries, keys, values, bias, heads):
    count, depth = queries.shape
    width = depth // heads
    own = (iota((heads, depth), 1) // width == iota((heads, depth), 0)).astype(f32)
    spread = (queries[:, None, :] * own[None]).reshape(count * heads, depth).astype(bf16)
    scores = lax.dot_general(spread, keys, NT, preferred_element_type=f32) * width ** (-0.5)
    scores = bias(scores)
    powers = jnp.exp(scores - jnp.max(scores, axis=-1, keepdims=True))
    weights = (powers * (1.0 / jnp.sum(powers, axis=-1, keepdims=True))).astype(bf16)
    mixed = dot(weights, values).reshape(count, heads, depth)
    return jnp.sum(mixed * own[None], axis=1)


def row_kernel(relative, side_relative, sides, lines, positions, *refs):
    terms, refs = refs[:sides], refs[sides:]
    blocks = refs[: len(refs) - 10]
    own, embedded, entry, leave, after, payload, bias, keys, values, mix = refs[len(refs) - 10 :]
    depth = leave.shape[0]
    heads = bias.shape[0] // positions
    rows = lines * positions
    key_count = bias.shape[1]
    me = lax.axis_index("res")
    lanes = terms[0].shape[1]
    per = lanes // positions
    side = side_index()
    sums = []
    for term in terms:
        held = positions * heads // per
        base = term.shape[0] - 3 * held
        sums.append(
            term[base : base + held, :].astype(f32)
            + term[base + held : base + 2 * held, :].astype(f32)
            + term[base + 2 * held :, :].astype(f32)
        )
    place = iota((heads, key_count), 1) // positions
    for line in range(positions):
        total = jnp.zeros((heads, key_count), f32)
        for slot, values_of in enumerate(sums):
            source = (side ^ slot) if side_relative else slot
            part = values_of[(line // per) * heads : (line // per + 1) * heads]
            part = pltpu.roll(part, ((source - line % per + lanes) % per) * positions, 1)
            part = jnp.concatenate([part] * (key_count // lanes), axis=1)
            total = jnp.where(place == source, part, total)
        bias[line * heads : (line + 1) * heads, :] = total
    penalty = jnp.zeros((payload.shape[0] - rows, key_count), f32)
    for slot, block in enumerate(blocks):
        source = (me ^ slot) if relative else slot
        place = iota((depth, key_count), 0)
        place = (place < positions) & (iota((depth, key_count), 1) == place + source * positions)
        penalty += dot(block[rows:, :], place.astype(bf16))
        projected = dot(block[:rows, :], entry[:, depth : 3 * depth]).astype(bf16)
        for line in range(lines):
            span = pl.ds(pl.multiple_of(source * positions, positions), positions)
            part = projected[line * positions : (line + 1) * positions]
            keys[line, span, :] = part[:, :depth]
            values[line, span, :] = part[:, depth:]
    penalty = masked_fill_value * (penalty - 1.0)
    normed = own[:rows, :]
    queries = dot(normed, entry[:, :depth]).astype(bf16).astype(f32)
    gate = sigmoid(dot(normed, entry[:, 3 * depth :]))
    for line in range(lines):
        span = slice(line * positions, (line + 1) * positions)
        fixed = lambda scores, line=line: scores + bias[...] + penalty[line : line + 1, :]
        mixed = attend(queries[span], keys[line], values[line], fixed, heads)
        mix[span, :] = (gate[span] * mixed).astype(bf16)
    result = embedded[...] + dot(mix[...], leave[...])
    after[...] = result
    payload[:rows, :] = normalize(result).astype(bf16)
    payload[rows:, :] = own[rows:, :]


def column_kernel(lines, positions, group, heads, *refs):
    blocks = refs[: len(refs) - 10]
    own, after, entry, leave, first, second, output, keys, values, mix = refs[len(refs) - 10 :]
    depth = leave.shape[0]
    rows = lines * positions
    presence = []
    blocks = [
        block.at[part] if len(block.shape) == 3 else block
        for block in blocks
        for part in range(block.shape[0] if len(block.shape) == 3 else 1)
    ]
    for slot, block in enumerate(blocks):
        projected = dot(block[:rows, :], entry[:, depth : 3 * depth])
        span = slice(slot * lines, (slot + 1) * lines)
        keys[span] = projected[:, :depth].reshape(lines, positions, depth)
        values[span] = projected[:, depth:].reshape(lines, positions, depth)
        presence.append(block[rows:, :])
    tail = presence[0].shape[0]
    presence = jnp.concatenate(presence, axis=0)
    normed = own[:rows, :]
    queries = dot(normed, entry[:, :depth]).astype(bf16).astype(f32)
    queries = queries.reshape(lines, positions, depth)
    gate = sigmoid(dot(normed, entry[:, 3 * depth :])).reshape(lines, positions, depth)
    key_count = len(blocks) * lines * group
    row = iota((presence.shape[0], key_count), 0)
    lane = iota((presence.shape[0], key_count), 1)
    chosen = (row % tail < lines) & ((row // tail) * lines + row % tail == lane // group)
    shape = (lines * group * heads, key_count)
    same = (iota(shape, 0) // heads) % group == iota(shape, 1) % group
    for start in range(0, positions, group):
        span = slice(start, start + group)
        pick = (iota((depth, key_count), 0) == start + iota((depth, key_count), 1) % group)
        held = dot(presence, pick.astype(bf16))
        held = jnp.sum(jnp.where(chosen, held, 0.0), axis=0, keepdims=True)
        penalty = masked_fill_value * (held - 1.0)
        fixed = lambda scores: jnp.where(same, scores + penalty, -jnp.inf)
        mixed = attend(
            queries[:, span].reshape(lines * group, depth),
            keys[:, span].reshape(key_count, depth).astype(bf16),
            values[:, span].reshape(key_count, depth).astype(bf16),
            fixed,
            heads,
        )
        mix[:, span] = gate[:, span] * mixed.reshape(lines, group, depth)
    mixed = mix[...].reshape(rows, depth).astype(bf16)
    result = after[...] + dot(mixed, leave[...])
    hidden = jnp.maximum(dot(normalize(result).astype(bf16), first[...]), 0.0).astype(bf16)
    result = result + dot(hidden, second[...])
    output[...] = result.astype(bf16).reshape(output.shape)


def fetch(sources, buffers, semaphores):
    copies = [
        pltpu.make_async_copy(source, buffer, semaphores.at[index])
        for index, (source, buffer) in enumerate(zip(sources, buffers))
    ]
    for copy in copies:
        copy.start()
    for copy in copies:
        copy.wait()


def split(values):
    high = values.astype(bf16)
    rest = values - high.astype(f32)
    middle = rest.astype(bf16)
    return high, middle, (rest - middle.astype(f32)).astype(bf16)


def start_kernel(count, present, *refs):
    sources, outputs, rest = refs[:count], refs[count : count + 6], refs[count + 6 :]
    buffers, semaphores, tail = rest[:count], rest[count], rest[count + 1]
    fetch(sources, buffers, semaphores)
    embedded, payload, gate, terms, near, left = outputs
    embed_kernel(*buffers[:4], embedded, payload, tail)
    present_row, pairs, entry, logits = buffers[4:]
    lines, positions, width = pairs.shape
    heads = logits.shape[0]
    normed = normalize(pairs[...].astype(f32).reshape(lines * positions, width)).astype(bf16)
    logit = lax.dot_general(logits[...], normed, NT, preferred_element_type=f32)
    held = terms.shape[0] // 3
    for index, term in enumerate(split(logit)):
        for part in range(held // heads):
            base = index * held + part * heads
            terms[base : base + heads, :] = term[:, part * width : (part + 1) * width]
    projected = dot(normed, entry[...])
    gate[...] = sigmoid(projected[:, 4 * width :])
    left[...] = (sigmoid(projected[:, width : 2 * width]) * projected[:, :width]).astype(bf16)
    operand = sigmoid(projected[:, 3 * width : 4 * width]) * projected[:, 2 * width : 3 * width]
    operand = operand.astype(bf16)
    mask_right(lax.axis_index("res"), operand, present, present_row, near)


def hold_kernel(left, terms, out):
    out[: left.shape[0], :] = left[...]
    out[left.shape[0] :, :] = terms[...]


def on_turn():
    return lax.axis_index("res") % 2 == lax.axis_index("aux")


def turn_kernel(pairs, entry, own, both, out):
    width = pairs.shape[2]
    operand = gated(pairs, entry[:, : 2 * width])
    area = operand.shape[0]
    both[:area, :] = jnp.where(on_turn(), own[:area, :].astype(f32), operand.astype(f32)).astype(
        bf16
    )
    both[area : 2 * area, :] = operand
    both[2 * area :, :] = own[area:, :]
    out[:area, :] = operand
    out[area:, :] = own[area:, :]


def gated(pairs, weight):
    lines, positions, width = pairs.shape
    normed = normalize(pairs[...].astype(f32).reshape(lines * positions, width)).astype(bf16)
    projected = dot(normed, weight)
    return (sigmoid(projected[:, width:]) * projected[:, :width]).astype(bf16)


def left_kernel(pairs, entry, left):
    width = pairs.shape[2]
    left[...] = gated(pairs, entry[:, : 2 * width])


def mask_right(source, operand, present, present_row, right):
    lines, positions, width = right.shape
    lane = iota((positions, present_row.shape[1]), 1)
    lane = lane == iota((positions, present_row.shape[1]), 0) + side_index() * positions
    valid = jnp.where(lane, present_row[...].astype(f32), 0.0)
    valid = jnp.sum(valid, axis=1, keepdims=True)
    operand = operand.astype(f32)
    for line in range(lines):
        both = valid * present[source * lines + line].astype(f32)
        right[line] = (operand[line * positions : (line + 1) * positions] * both).astype(
            right.dtype
        )


def right_operand(relative, slot, present, present_row, pairs, entry, right):
    width = pairs.shape[2]
    source = (lax.axis_index("res") ^ slot) if relative else slot
    operand = gated(pairs, entry[:, 2 * width : 4 * width])
    mask_right(source, operand, present, present_row, right)


def pick_left(relative, slot, lefts, left):
    source = (lax.axis_index("res") ^ slot) if relative[0] else slot
    side = side_index()
    for place, block in enumerate(lefts):
        held = (side ^ place) if relative[1] else place

        @pl.when(held == source)
        def _():
            left[...] = block[...].astype(f32).reshape(left.shape)


def accumulate(left, right, total_in, total):
    step = 4
    depth, positions, width = right.shape

    def body(index, carry):
        base = index * step
        sums = [None if total_in is None else total_in[base + t] for t in range(step)]
        for line in range(depth):
            line_right = right[line].astype(f32)
            for t in range(step):
                term = left[line, pl.ds(base + t, 1), :] * line_right
                sums[t] = term if sums[t] is None else sums[t] + term
        for t in range(step):
            total[base + t] = sums[t]
        return carry

    lax.fori_loop(0, total.shape[0] // step, body, 0)


def middle_kernel(relative, slots, *refs):
    rights, lefts = refs[: len(slots)], refs[len(slots) : -2]
    total, left = refs[-2:]
    for index, slot in enumerate(slots):
        pick_left(relative, slot, lefts, left)
        accumulate(left, rights[index], total if index else None, total)


def last_kernel(relative, slot, *refs):
    present, present_row, pairs, entry, total_in, own, gate, leave = refs[:8]
    lefts, (out, left, right, total) = refs[8:-4], refs[-4:]
    lines, positions, width = out.shape
    pick_left(relative, slot, lefts, left)
    right_operand(relative[0], slot, present, present_row, pairs, entry, right)
    accumulate(left, right, total_in, total)
    me = lax.axis_index("res")
    for line in range(lines):
        total[line] = total[line] * present[me * lines + line].astype(f32)
    product = total[...].reshape(lines * positions, width).astype(bf16).astype(f32)
    update = gate[...] * dot(normalize(product).astype(bf16), leave[...])
    out[...] = (own[...].astype(f32) + update.reshape(out.shape)).astype(bf16)


def far_kernel(present, present_row, turned, crossed, entry, right):
    width = turned.shape[2]
    pairs = jnp.where(on_turn(), turned[...].astype(f32), crossed[...].astype(f32))
    operand = gated(pairs, entry[:, 2 * width : 4 * width])
    mask_right(lax.axis_index("res") ^ 1, operand, present, present_row, right)


def accumulate_rows(left, right, total_in, total):
    step = 8

    def body(index, carry):
        base = index * step
        sums = [None if total_in is None else total_in[base + t] for t in range(step)]
        for line in range(right.shape[0]):
            line_right = right[line]
            for t in range(step):
                term = left[line, pl.ds(base + t, 1), :] * line_right
                sums[t] = term if sums[t] is None else sums[t] + term
        for t in range(step):
            total[base + t] = sums[t].astype(total.dtype)
        return carry

    lax.fori_loop(0, total.shape[0] // step, body, 0)


def load_left(block, base, left):
    lines, count, _ = left.shape
    for line in range(lines):
        start = base + line * count
        left[line] = block[start : start + count, :].astype(f32)


def early_kernel(other_half, own, other, near, sums, left):
    same = lax.axis_index("br") == lax.axis_index("res") // 2
    mine = jnp.logical_not(same) if other_half else same
    pl.when(mine)(lambda: load_left(own, 0, left))
    pl.when(jnp.logical_not(mine))(lambda: load_left(other, 0, left))
    accumulate_rows(left, near, None, sums)


def late_kernel(other_half, came, passed, other_came, other_passed, far, sums, total, left):
    same = lax.axis_index("br") == lax.axis_index("res") // 2
    mine = jnp.logical_not(same) if other_half else same
    turn = on_turn()
    other, straight = jnp.logical_not(mine), jnp.logical_not(turn)
    area = left.shape[0] * left.shape[1]
    pl.when(mine & turn)(lambda: load_left(came, 0, left))
    pl.when(mine & straight)(lambda: load_left(passed, 0, left))
    pl.when(other & turn)(lambda: load_left(other_came, area, left))
    pl.when(other & straight)(lambda: load_left(other_passed, 0, left))
    accumulate_rows(left, far, sums, total)


def finish_kernel(present, kept, own, gate, leave, *refs):
    received, (out, total) = refs[:-2], refs[-2:]
    lines, positions, width = out.shape
    me = lax.axis_index("res")
    each = lines // len(received)
    for line in range(lines):
        sums = kept[line] + received[line // each][line % each].astype(f32)
        total[line] = sums * present[me * lines + line].astype(f32)
    product = total[...].reshape(lines * positions, width).astype(bf16).astype(f32)
    update = gate[...] * dot(normalize(product).astype(bf16), leave[...])
    out[...] = (own[...].astype(f32) + update.reshape(out.shape)).astype(bf16)


def gather(block, axis):
    size = lax.axis_size(axis)
    if size in (1, 2, 4):
        return [block] + [flip(block, axis, d) for d in range(1, size)], True
    whole = lax.all_gather(block, axis)
    return [whole[i] for i in range(size)], False


def flip(block, axis, bit=1):
    return lax.ppermute(block, axis, [(i, i ^ bit) for i in range(lax.axis_size(axis))])


def gather_side(block):
    if lax.axis_size("br") == 2 and lax.axis_size("aux") == 2:
        near = flip(block, "br")
        far = flip(block, "aux")
        return [block, far, near, flip(far, "br")], True
    whole = lax.all_gather(block, SIDE)
    return [whole[i] for i in range(whole.shape[0])], False


def pair_up(block, other, out):
    out[0] = block[...]
    out[1] = other[...]


def double(block, axis, bit, axis_after, ahead):
    far = flip(block, axis, bit)
    pair = call(pair_up, shape((2, *block.shape), block.dtype), after=ahead)(block, far)
    return [pair, flip(pair, axis_after)]


def double_side(block, ahead):
    return double(block, "aux", 1, "br", ahead)


def shape(dims, kind):
    return jax.ShapeDtypeStruct(dims, kind)


def call(kernel, out_shape, scratch=(), smem=0, after=(), hbm=False):
    def run(*args):
        count, unread = len(args), len(after)

        def ordered(*refs):
            kernel(*refs[:count], *refs[count + unread :])

        return pl.pallas_call(
            ordered,
            out_shape=out_shape,
            in_specs=[pl.BlockSpec(memory_space=pltpu.SMEM)] * smem
            + [pl.BlockSpec(memory_space=pltpu.HBM if hbm else pltpu.VMEM)] * (count - smem)
            + [pl.BlockSpec(memory_space=pl.ANY)] * unread,
            out_specs=jax.tree.map(lambda _: pl.BlockSpec(memory_space=pltpu.VMEM), out_shape),
            scratch_shapes=list(scratch),
            compiler_params=pltpu.CompilerParams(vmem_limit_bytes=(62 if hbm else 48) * 1024 * 1024),
            cost_estimate=pl.CostEstimate(flops=1, bytes_accessed=1, transcendentals=0),
        )(*args, *after)

    return run


def triangle_by_gather(pairs, presence, entry, leave, gate):
    res = lax.axis_size("res")
    side = lax.axis_size("br") * lax.axis_size("aux")
    rows, cols, width = pairs.shape
    cube = pltpu.VMEM((rows, cols, width), f32)
    turned = lax.ppermute(
        pairs, ALL, [(r * side + b, b * side + r) for r in range(res) for b in range(side)]
    )
    left = call(left_kernel, shape((rows * cols, width), bf16))(turned, entry)
    lefts, left_relative = gather_side(left)
    blocks, pair_relative = gather(pairs, "res")
    relative = (pair_relative, left_relative)
    slots = list(range(res - 1))
    rights = [
        call(
            functools.partial(right_operand, pair_relative, slot), shape(pairs.shape, bf16), smem=1
        )(*presence, blocks[slot], entry)
        for slot in slots
    ]
    total = call(
        functools.partial(middle_kernel, relative, slots), shape(pairs.shape, f32), [cube]
    )(*rights, *lefts)
    return call(
        functools.partial(last_kernel, relative, res - 1),
        shape(pairs.shape, bf16),
        [cube, cube, cube],
        smem=1,
    )(*presence, blocks[-1], entry, total, pairs, gate, leave, *lefts)


def turn_pairs(pairs):
    index = lambda half, low, br, aux: ((half * 2 + low) * 2 + br) * 2 + aux
    every = [(h, low, br, aux) for h in (0, 1) for low in (0, 1) for br in (0, 1) for aux in (0, 1)]
    goes = lambda h, l, br, a: index(h, l, br, 1 - a) if a == l else index(h, 1 - l, br, a)
    turned = lax.ppermute(pairs, ALL, [(index(*place), goes(*place)) for place in every])
    crossed = lax.ppermute(
        pairs, ALL, [(index(h, l, br, a), index(h, 1 - l, br, a)) for h, l, br, a in every if a == l]
    )
    return turned, crossed


def on_device(
    homolog_features,
    couple_features,
    symbol_ids,
    entry_present,
    amino_present,
    symbol_lookup_matrix,
    horizontal_entry_matrix,
    couple_logit_matrix,
    horizontal_exit_matrix,
    vertical_entry_matrix,
    vertical_exit_matrix,
    feedforward_first_matrix,
    feedforward_second_matrix,
    trimul_entry_matrix,
    trimul_exit_matrix,
):
    lines, positions, depth = homolog_features.shape
    pair_rows, pair_cols, width = couple_features.shape
    heads = couple_logit_matrix.shape[1]
    res = lax.axis_size("res")
    side = lax.axis_size("br") * lax.axis_size("aux")
    rows = lines * positions
    tail = round_up(lines, 16)
    residues = positions * res
    area = pair_rows * pair_cols
    held = pair_rows * pair_cols * heads // width
    presence = [amino_present, amino_present[None, :]]
    halves = (res, lax.axis_size("br"), lax.axis_size("aux")) == (4, 2, 2)

    args = (
        homolog_features,
        symbol_ids,
        entry_present,
        symbol_lookup_matrix,
        amino_present[None, :],
        couple_features,
        trimul_entry_matrix,
        couple_logit_matrix.T,
    )
    embedded, payload, gate, terms, near, left = call(
        functools.partial(start_kernel, len(args)),
        (
            shape((rows, depth), f32),
            shape((rows + tail, depth), bf16),
            shape((area, width), f32),
            shape((3 * held, width), bf16),
            shape(couple_features.shape, f32),
            shape((area, width), bf16),
        ),
        [pltpu.VMEM(x.shape, x.dtype) for x in args]
        + [pltpu.SemaphoreType.DMA((len(args),)), pltpu.VMEM((tail, depth), f32)],
        smem=1,
        hbm=True,
    )(amino_present, *args)
    pending = ()
    if halves:
        row_blocks, row_relative = gather(payload, "res")
        turned, crossed = turn_pairs(couple_features)
        turned, crossed = lax.optimization_barrier((turned, crossed))
        held_left = call(hold_kernel, shape((area + 3 * held, width), bf16))(left, terms)
        both, came = call(
            turn_kernel,
            (shape((2 * area + 3 * held, width), bf16), shape((area + 3 * held, width), bf16)),
        )(turned, trimul_entry_matrix, held_left)
        passed = flip(came, "aux")
        other = flip(both, "br")
        cube = shape(couple_features.shape, f32)
        scratch = [pltpu.VMEM(couple_features.shape, f32)]
        far = call(far_kernel, cube, smem=1)(*presence, turned, crossed, trimul_entry_matrix)
        nearest = lax.optimization_barrier((near, far))[0]
        early = lambda other_half, right: call(
            functools.partial(early_kernel, other_half), cube, scratch
        )(both, other, right)
        sent = early(True, nearest)
        ready = lax.optimization_barrier((passed, far, sent, *row_blocks[1:]))[0]
        other_passed = flip(ready, "br")
        operands = (came, passed, other, other_passed, far)
        terms, side_relative = (came, passed, other, other_passed), True
        late = lambda other_half, kind, sums, after: call(
            functools.partial(late_kernel, other_half),
            shape(couple_features.shape, kind),
            scratch,
            after=after,
        )(*operands, sums)
        sent = late(True, bf16, sent, ())
        received = flip(sent, "res", 2)
        pending = (sent,)
    else:
        row_blocks, row_relative = gather(payload, "res")
        terms, side_relative = gather_side(terms)

    after, payload = call(
        functools.partial(row_kernel, row_relative, side_relative, side, lines, positions),
        (shape((rows, depth), f32), shape((rows + tail, depth), bf16)),
        [
            pltpu.VMEM((pair_rows * heads, residues), f32),
            pltpu.VMEM((lines, residues, depth), bf16),
            pltpu.VMEM((lines, residues, depth), bf16),
            pltpu.VMEM((rows, depth), bf16),
        ],
        after=pending,
    )(*terms, *row_blocks, payload, embedded, horizontal_entry_matrix, horizontal_exit_matrix)
    if halves:
        kept = early(False, lax.optimization_barrier((near, payload))[0])
        column_blocks = double_side(payload, (kept,))
        kept = late(False, f32, kept, ())
        pending = (kept,)
    else:
        column_blocks = gather_side(payload)[0]
    group = 8
    alignment_output = call(
        functools.partial(column_kernel, lines, positions, group, heads),
        shape((lines, positions, depth), bf16),
        [
            pltpu.VMEM((side * lines, positions, depth), f32),
            pltpu.VMEM((side * lines, positions, depth), f32),
            pltpu.VMEM((lines, positions, depth), f32),
        ],
        after=pending,
    )(
        *column_blocks,
        payload,
        after,
        vertical_entry_matrix,
        vertical_exit_matrix,
        feedforward_first_matrix,
        feedforward_second_matrix,
    )
    if halves:
        pair_output = call(
            finish_kernel,
            shape(couple_features.shape, bf16),
            [pltpu.VMEM(couple_features.shape, f32)],
            smem=1,
        )(amino_present, kept, couple_features, gate, trimul_exit_matrix, received)
    else:
        pair_output = triangle_by_gather(
            couple_features, presence, trimul_entry_matrix, trimul_exit_matrix, gate
        )
    return (alignment_output, pair_output)


def solution(mesh):
    return jax.shard_map(
        on_device,
        mesh=mesh,
        in_specs=(
            P(("grp", "br", "aux"), "res", None),
            P(("grp", "res"), ("br", "aux"), None),
            P(("grp", "br", "aux"), "res"),
            P(("grp", "br", "aux"), "res"),
            P("grp"),
            P(),
            P(),
            P(),
            P(),
            P(),
            P(),
            P(),
            P(),
            P(),
            P(),
        ),
        out_specs=(P(("grp", "br", "aux"), "res", None), P(("grp", "res"), ("br", "aux"), None)),
        check_vma=False,
    )
```

```python
import functools

import jax
import jax.numpy as jnp
from jax import lax
from jax.experimental import pallas as pl
from jax.experimental.pallas import tpu as pltpu
from jax.sharding import PartitionSpec as P

epsilon = 1e-05
masked_fill_value = 1000000000.0
bf16 = jnp.bfloat16
f32 = jnp.float32
SIDE = ("br", "aux")
ALL = ("res", "br", "aux")
NT = (((1,), (1,)), ((), ()))
TN = (((0,), (0,)), ((), ()))


def normalize(values):
    average = jnp.mean(values, axis=-1, keepdims=True)
    centred = values - average
    variance = jnp.mean(centred * centred, axis=-1, keepdims=True)
    return centred * lax.rsqrt(variance + epsilon)


def sigmoid(values):
    return 1.0 / (1.0 + jnp.exp(-values))


def dot(left, right):
    return jnp.dot(left, right, preferred_element_type=f32)


def iota(shape, dim):
    return lax.broadcasted_iota(jnp.int32, shape, dim)


def round_up(count, step):
    return -(-count // step) * step


def side_index():
    return lax.axis_index("br") * lax.axis_size("aux") + lax.axis_index("aux")


def embed_kernel(features, ids, present, table, embedded, payload, tail):
    lines, positions, depth = features.shape
    kinds = table.shape[0]
    rows = lines * positions
    for line in range(lines):
        onehot = (iota((kinds, positions), 0) == ids[line : line + 1, :]).astype(bf16)
        token = lax.dot_general(onehot, table[...], TN, preferred_element_type=f32)
        values = features[line].astype(f32) + token
        span = slice(line * positions, (line + 1) * positions)
        embedded[span, :] = values
        payload[span, :] = normalize(values).astype(bf16)
    tail[...] = jnp.zeros_like(tail)
    tail[:lines, :positions] = present[...].astype(f32)
    payload[rows:, :] = tail[...].astype(bf16)


def attend(queries, keys, values, bias, heads):
    count, depth = queries.shape
    width = depth // heads
    own = (iota((heads, depth), 1) // width == iota((heads, depth), 0)).astype(f32)
    spread = (queries[:, None, :] * own[None]).reshape(count * heads, depth).astype(bf16)
    scores = lax.dot_general(spread, keys, NT, preferred_element_type=f32) * width ** (-0.5)
    scores = bias(scores)
    powers = jnp.exp(scores - jnp.max(scores, axis=-1, keepdims=True))
    weights = (powers * (1.0 / jnp.sum(powers, axis=-1, keepdims=True))).astype(bf16)
    mixed = dot(weights, values).reshape(count, heads, depth)
    return jnp.sum(mixed * own[None], axis=1)


def row_kernel(relative, side_relative, places, lines, positions, *refs):
    used = 1 + max(max(index, index if other is None else other) for index, _, other in places)
    terms, refs = refs[:used], refs[used:]
    blocks = refs[: len(refs) - 10]
    own, embedded, entry, leave, after, payload, bias, keys, values, mix = refs[len(refs) - 10 :]
    depth = leave.shape[0]
    heads = bias.shape[0] // positions
    rows = lines * positions
    key_count = bias.shape[1]
    me = lax.axis_index("res")
    lanes = terms[0].shape[1]
    per = lanes // positions
    side = side_index()
    sums = []
    held = positions * heads // per
    sums = []
    for source, start, other in places:
        parts = []
        for index in range(3):
            first = index * held
            part = terms[source][start + first : start + first + held, :].astype(f32)
            if other is not None:
                choice = terms[other][first : first + held, :].astype(f32)
                part = jnp.where(on_turn(), choice, part)
            parts.append(part)
        sums.append(parts[0] + parts[1] + parts[2])
    place = iota((heads, key_count), 1) // positions
    for line in range(positions):
        total = jnp.zeros((heads, key_count), f32)
        for slot, values_of in enumerate(sums):
            source = (side ^ slot) if side_relative else slot
            part = values_of[(line // per) * heads : (line // per + 1) * heads]
            part = pltpu.roll(part, ((source - line % per + lanes) % per) * positions, 1)
            part = jnp.concatenate([part] * (key_count // lanes), axis=1)
            total = jnp.where(place == source, part, total)
        bias[line * heads : (line + 1) * heads, :] = total
    penalty = jnp.zeros((payload.shape[0] - rows, key_count), f32)
    for slot, block in enumerate(blocks):
        source = (me ^ slot) if relative else slot
        place = iota((depth, key_count), 0)
        place = (place < positions) & (iota((depth, key_count), 1) == place + source * positions)
        penalty += dot(block[rows:, :], place.astype(bf16))
        projected = dot(block[:rows, :], entry[:, depth : 3 * depth]).astype(bf16)
        for line in range(lines):
            span = pl.ds(pl.multiple_of(source * positions, positions), positions)
            part = projected[line * positions : (line + 1) * positions]
            keys[line, span, :] = part[:, :depth]
            values[line, span, :] = part[:, depth:]
    penalty = masked_fill_value * (penalty - 1.0)
    normed = own[:rows, :]
    queries = dot(normed, entry[:, :depth]).astype(bf16).astype(f32)
    gate = sigmoid(dot(normed, entry[:, 3 * depth :]))
    for line in range(lines):
        span = slice(line * positions, (line + 1) * positions)
        fixed = lambda scores, line=line: scores + bias[...] + penalty[line : line + 1, :]
        mixed = attend(queries[span], keys[line], values[line], fixed, heads)
        mix[span, :] = (gate[span] * mixed).astype(bf16)
    result = embedded[...] + dot(mix[...], leave[...])
    after[...] = result
    payload[:rows, :] = normalize(result).astype(bf16)
    payload[rows:, :] = own[rows:, :]


def column_kernel(lines, positions, group, heads, *refs):
    blocks = refs[: len(refs) - 10]
    own, after, entry, leave, first, second, output, keys, values, mix = refs[len(refs) - 10 :]
    depth = leave.shape[0]
    rows = lines * positions
    presence = []
    blocks = [
        block.at[part] if len(block.shape) == 3 else block
        for block in blocks
        for part in range(block.shape[0] if len(block.shape) == 3 else 1)
    ]
    for slot, block in enumerate(blocks):
        projected = dot(block[:rows, :], entry[:, depth : 3 * depth])
        span = slice(slot * lines, (slot + 1) * lines)
        keys[span] = projected[:, :depth].reshape(lines, positions, depth)
        values[span] = projected[:, depth:].reshape(lines, positions, depth)
        presence.append(block[rows:, :])
    tail = presence[0].shape[0]
    presence = jnp.concatenate(presence, axis=0)
    normed = own[:rows, :]
    queries = dot(normed, entry[:, :depth]).astype(bf16).astype(f32)
    queries = queries.reshape(lines, positions, depth)
    gate = sigmoid(dot(normed, entry[:, 3 * depth :])).reshape(lines, positions, depth)
    key_count = len(blocks) * lines * group
    row = iota((presence.shape[0], key_count), 0)
    lane = iota((presence.shape[0], key_count), 1)
    chosen = (row % tail < lines) & ((row // tail) * lines + row % tail == lane // group)
    shape = (lines * group * heads, key_count)
    same = (iota(shape, 0) // heads) % group == iota(shape, 1) % group
    for start in range(0, positions, group):
        span = slice(start, start + group)
        pick = (iota((depth, key_count), 0) == start + iota((depth, key_count), 1) % group)
        held = dot(presence, pick.astype(bf16))
        held = jnp.sum(jnp.where(chosen, held, 0.0), axis=0, keepdims=True)
        penalty = masked_fill_value * (held - 1.0)
        fixed = lambda scores: jnp.where(same, scores + penalty, -jnp.inf)
        mixed = attend(
            queries[:, span].reshape(lines * group, depth),
            keys[:, span].reshape(key_count, depth).astype(bf16),
            values[:, span].reshape(key_count, depth).astype(bf16),
            fixed,
            heads,
        )
        mix[:, span] = gate[:, span] * mixed.reshape(lines, group, depth)
    mixed = mix[...].reshape(rows, depth).astype(bf16)
    result = after[...] + dot(mixed, leave[...])
    hidden = jnp.maximum(dot(normalize(result).astype(bf16), first[...]), 0.0).astype(bf16)
    result = result + dot(hidden, second[...])
    output[...] = result.astype(bf16).reshape(output.shape)


def fetch(sources, buffers, semaphores):
    copies = [
        pltpu.make_async_copy(source, buffer, semaphores.at[index])
        for index, (source, buffer) in enumerate(zip(sources, buffers))
    ]
    for copy in copies:
        copy.start()
    for copy in copies:
        copy.wait()


def split(values):
    high = values.astype(bf16)
    rest = values - high.astype(f32)
    middle = rest.astype(bf16)
    return high, middle, (rest - middle.astype(f32)).astype(bf16)


def store_terms(logit, out, start):
    heads, count = logit.shape
    lanes = out.shape[1]
    for index, term in enumerate(split(logit)):
        for part in range(count // lanes):
            base = start + (index * (count // lanes) + part) * heads
            out[base : base + heads, :] = term[:, part * lanes : (part + 1) * lanes]


def start_kernel(count, present, *refs):
    sources, outputs, rest = refs[:count], refs[count : count + 6], refs[count + 6 :]
    buffers, semaphores, tail = rest[:count], rest[count], rest[count + 1]
    fetch(sources, buffers, semaphores)
    embedded, payload, gate, terms, near, left = outputs
    embed_kernel(*buffers[:4], embedded, payload, tail)
    present_row, pairs, entry, logits = buffers[4:]
    lines, positions, width = pairs.shape
    heads = logits.shape[0]
    normed = normalize(pairs[...].astype(f32).reshape(lines * positions, width)).astype(bf16)
    logit = lax.dot_general(logits[...], normed, NT, preferred_element_type=f32)
    store_terms(logit, terms, 0)
    projected = dot(normed, entry[...])
    gate[...] = sigmoid(projected[:, 4 * width :])
    left[...] = (sigmoid(projected[:, width : 2 * width]) * projected[:, :width]).astype(bf16)
    operand = sigmoid(projected[:, 3 * width : 4 * width]) * projected[:, 2 * width : 3 * width]
    operand = operand.astype(bf16)
    mask_right(lax.axis_index("res"), operand, present, present_row, near)


def on_turn():
    return lax.axis_index("res") % 2 == lax.axis_index("aux")


def turn_kernel(pairs, entry, logits, terms, came, given, both):
    lines, positions, width = pairs.shape
    held = terms.shape[0]
    normed = normalize(pairs[...].astype(f32).reshape(lines * positions, width)).astype(bf16)
    projected = dot(normed, entry[:, : 2 * width])
    operand = (sigmoid(projected[:, width:]) * projected[:, :width]).astype(bf16)
    came[...] = operand
    given[...] = operand

    @pl.when(jnp.logical_not(on_turn()))
    def _():
        given[:held, :] = terms[...]

    both[:held, :] = terms[...]
    logit = lax.dot_general(logits[...], normed, NT, preferred_element_type=f32)
    store_terms(logit, both, held)


def gated(pairs, weight):
    lines, positions, width = pairs.shape
    normed = normalize(pairs[...].astype(f32).reshape(lines * positions, width)).astype(bf16)
    projected = dot(normed, weight)
    return (sigmoid(projected[:, width:]) * projected[:, :width]).astype(bf16)


def left_kernel(pairs, entry, left):
    width = pairs.shape[2]
    left[...] = gated(pairs, entry[:, : 2 * width])


def mask_right(source, operand, present, present_row, right):
    lines, positions, width = right.shape
    lane = iota((positions, present_row.shape[1]), 1)
    lane = lane == iota((positions, present_row.shape[1]), 0) + side_index() * positions
    valid = jnp.where(lane, present_row[...].astype(f32), 0.0)
    valid = jnp.sum(valid, axis=1, keepdims=True)
    operand = operand.astype(f32)
    for line in range(lines):
        both = valid * present[source * lines + line].astype(f32)
        right[line] = (operand[line * positions : (line + 1) * positions] * both).astype(
            right.dtype
        )


def right_operand(relative, slot, present, present_row, pairs, entry, right):
    width = pairs.shape[2]
    source = (lax.axis_index("res") ^ slot) if relative else slot
    operand = gated(pairs, entry[:, 2 * width : 4 * width])
    mask_right(source, operand, present, present_row, right)


def pick_left(relative, slot, lefts, left):
    source = (lax.axis_index("res") ^ slot) if relative[0] else slot
    side = side_index()
    for place, block in enumerate(lefts):
        held = (side ^ place) if relative[1] else place

        @pl.when(held == source)
        def _():
            left[...] = block[...].astype(f32).reshape(left.shape)


def accumulate(left, right, total_in, total):
    step = 4
    depth, positions, width = right.shape

    def body(index, carry):
        base = index * step
        sums = [None if total_in is None else total_in[base + t] for t in range(step)]
        for line in range(depth):
            line_right = right[line].astype(f32)
            for t in range(step):
                term = left[line, pl.ds(base + t, 1), :] * line_right
                sums[t] = term if sums[t] is None else sums[t] + term
        for t in range(step):
            total[base + t] = sums[t]
        return carry

    lax.fori_loop(0, total.shape[0] // step, body, 0)


def middle_kernel(relative, slots, *refs):
    rights, lefts = refs[: len(slots)], refs[len(slots) : -2]
    total, left = refs[-2:]
    for index, slot in enumerate(slots):
        pick_left(relative, slot, lefts, left)
        accumulate(left, rights[index], total if index else None, total)


def last_kernel(relative, slot, *refs):
    present, present_row, pairs, entry, total_in, own, gate, leave = refs[:8]
    lefts, (out, left, right, total) = refs[8:-4], refs[-4:]
    lines, positions, width = out.shape
    pick_left(relative, slot, lefts, left)
    right_operand(relative[0], slot, present, present_row, pairs, entry, right)
    accumulate(left, right, total_in, total)
    me = lax.axis_index("res")
    for line in range(lines):
        total[line] = total[line] * present[me * lines + line].astype(f32)
    product = total[...].reshape(lines * positions, width).astype(bf16).astype(f32)
    update = gate[...] * dot(normalize(product).astype(bf16), leave[...])
    out[...] = (own[...].astype(f32) + update.reshape(out.shape)).astype(bf16)


def far_kernel(present, present_row, turned, crossed, entry, right):
    width = turned.shape[2]
    pairs = jnp.where(on_turn(), turned[...].astype(f32), crossed[...].astype(f32))
    operand = gated(pairs, entry[:, 2 * width : 4 * width])
    mask_right(lax.axis_index("res") ^ 1, operand, present, present_row, right)


def accumulate_rows(left, right, total_in, total):
    step = 8

    def body(index, carry):
        base = index * step
        sums = [None if total_in is None else total_in[base + t] for t in range(step)]
        for line in range(right.shape[0]):
            line_right = right[line]
            for t in range(step):
                term = left[line, pl.ds(base + t, 1), :] * line_right
                sums[t] = term if sums[t] is None else sums[t] + term
        for t in range(step):
            total[base + t] = sums[t].astype(total.dtype)
        return carry

    lax.fori_loop(0, total.shape[0] // step, body, 0)


def load_left(block, base, left):
    lines, count, _ = left.shape
    for line in range(lines):
        start = base + line * count
        left[line] = block[start : start + count, :].astype(f32)


def early_kernel(other_half, own, came, other_own, other_came, near, sums, left):
    same = lax.axis_index("br") == lax.axis_index("res") // 2
    mine = jnp.logical_not(same) if other_half else same
    turn = on_turn()
    other, straight = jnp.logical_not(mine), jnp.logical_not(turn)
    pl.when(mine & turn)(lambda: load_left(own, 0, left))
    pl.when(mine & straight)(lambda: load_left(came, 0, left))
    pl.when(other & turn)(lambda: load_left(other_own, 0, left))
    pl.when(other & straight)(lambda: load_left(other_came, 0, left))
    accumulate_rows(left, near, None, sums)


def late_kernel(other_half, came, passed, other_came, other_passed, far, sums, total, left):
    same = lax.axis_index("br") == lax.axis_index("res") // 2
    mine = jnp.logical_not(same) if other_half else same
    turn = on_turn()
    other, straight = jnp.logical_not(mine), jnp.logical_not(turn)
    pl.when(mine & turn)(lambda: load_left(came, 0, left))
    pl.when(mine & straight)(lambda: load_left(passed, 0, left))
    pl.when(other & turn)(lambda: load_left(other_came, 0, left))
    pl.when(other & straight)(lambda: load_left(other_passed, 0, left))
    accumulate_rows(left, far, sums, total)


def finish_kernel(present, kept, own, gate, leave, *refs):
    received, (out, total) = refs[:-2], refs[-2:]
    lines, positions, width = out.shape
    me = lax.axis_index("res")
    each = lines // len(received)
    for line in range(lines):
        sums = kept[line] + received[line // each][line % each].astype(f32)
        total[line] = sums * present[me * lines + line].astype(f32)
    product = total[...].reshape(lines * positions, width).astype(bf16).astype(f32)
    update = gate[...] * dot(normalize(product).astype(bf16), leave[...])
    out[...] = (own[...].astype(f32) + update.reshape(out.shape)).astype(bf16)


def gather(block, axis):
    size = lax.axis_size(axis)
    if size in (1, 2, 4):
        return [block] + [flip(block, axis, d) for d in range(1, size)], True
    whole = lax.all_gather(block, axis)
    return [whole[i] for i in range(size)], False


def flip(block, axis, bit=1):
    return lax.ppermute(block, axis, [(i, i ^ bit) for i in range(lax.axis_size(axis))])


def gather_side(block):
    if lax.axis_size("br") == 2 and lax.axis_size("aux") == 2:
        near = flip(block, "br")
        far = flip(block, "aux")
        return [block, far, near, flip(far, "br")], True
    whole = lax.all_gather(block, SIDE)
    return [whole[i] for i in range(whole.shape[0])], False


def pair_up(block, other, out):
    out[0] = block[...]
    out[1] = other[...]


def double(block, axis, bit, axis_after, ahead):
    far = flip(block, axis, bit)
    pair = call(pair_up, shape((2, *block.shape), block.dtype), after=ahead)(block, far)
    return [pair, flip(pair, axis_after)]


def double_side(block, ahead):
    return double(block, "aux", 1, "br", ahead)


def shape(dims, kind):
    return jax.ShapeDtypeStruct(dims, kind)


def call(kernel, out_shape, scratch=(), smem=0, after=(), hbm=False):
    def run(*args):
        count, unread = len(args), len(after)

        def ordered(*refs):
            kernel(*refs[:count], *refs[count + unread :])

        return pl.pallas_call(
            ordered,
            out_shape=out_shape,
            in_specs=[pl.BlockSpec(memory_space=pltpu.SMEM)] * smem
            + [pl.BlockSpec(memory_space=pltpu.HBM if hbm else pltpu.VMEM)] * (count - smem)
            + [pl.BlockSpec(memory_space=pl.ANY)] * unread,
            out_specs=jax.tree.map(lambda _: pl.BlockSpec(memory_space=pltpu.VMEM), out_shape),
            scratch_shapes=list(scratch),
            compiler_params=pltpu.CompilerParams(vmem_limit_bytes=(62 if hbm else 48) * 1024 * 1024),
            cost_estimate=pl.CostEstimate(flops=1, bytes_accessed=1, transcendentals=0),
        )(*args, *after)

    return run


def triangle_by_gather(pairs, presence, entry, leave, gate):
    res = lax.axis_size("res")
    side = lax.axis_size("br") * lax.axis_size("aux")
    rows, cols, width = pairs.shape
    cube = pltpu.VMEM((rows, cols, width), f32)
    turned = lax.ppermute(
        pairs, ALL, [(r * side + b, b * side + r) for r in range(res) for b in range(side)]
    )
    left = call(left_kernel, shape((rows * cols, width), bf16))(turned, entry)
    lefts, left_relative = gather_side(left)
    blocks, pair_relative = gather(pairs, "res")
    relative = (pair_relative, left_relative)
    slots = list(range(res - 1))
    rights = [
        call(
            functools.partial(right_operand, pair_relative, slot), shape(pairs.shape, bf16), smem=1
        )(*presence, blocks[slot], entry)
        for slot in slots
    ]
    total = call(
        functools.partial(middle_kernel, relative, slots), shape(pairs.shape, f32), [cube]
    )(*rights, *lefts)
    return call(
        functools.partial(last_kernel, relative, res - 1),
        shape(pairs.shape, bf16),
        [cube, cube, cube],
        smem=1,
    )(*presence, blocks[-1], entry, total, pairs, gate, leave, *lefts)


def turn_pairs(pairs):
    index = lambda half, low, br, aux: ((half * 2 + low) * 2 + br) * 2 + aux
    every = [(h, low, br, aux) for h in (0, 1) for low in (0, 1) for br in (0, 1) for aux in (0, 1)]
    goes = lambda h, l, br, a: index(h, l, br, 1 - a) if a == l else index(h, 1 - l, br, a)
    turned = lax.ppermute(pairs, ALL, [(index(*place), goes(*place)) for place in every])
    crossed = lax.ppermute(
        pairs, ALL, [(index(h, l, br, a), index(h, 1 - l, br, a)) for h, l, br, a in every if a == l]
    )
    return turned, crossed


def on_device(
    homolog_features,
    couple_features,
    symbol_ids,
    entry_present,
    amino_present,
    symbol_lookup_matrix,
    horizontal_entry_matrix,
    couple_logit_matrix,
    horizontal_exit_matrix,
    vertical_entry_matrix,
    vertical_exit_matrix,
    feedforward_first_matrix,
    feedforward_second_matrix,
    trimul_entry_matrix,
    trimul_exit_matrix,
):
    lines, positions, depth = homolog_features.shape
    pair_rows, pair_cols, width = couple_features.shape
    heads = couple_logit_matrix.shape[1]
    res = lax.axis_size("res")
    side = lax.axis_size("br") * lax.axis_size("aux")
    rows = lines * positions
    tail = round_up(lines, 16)
    residues = positions * res
    area = pair_rows * pair_cols
    held = pair_rows * pair_cols * heads // width
    presence = [amino_present, amino_present[None, :]]
    halves = (res, lax.axis_size("br"), lax.axis_size("aux")) == (4, 2, 2)

    args = (
        homolog_features,
        symbol_ids,
        entry_present,
        symbol_lookup_matrix,
        amino_present[None, :],
        couple_features,
        trimul_entry_matrix,
        couple_logit_matrix.T,
    )
    embedded, payload, gate, terms, near, left = call(
        functools.partial(start_kernel, len(args)),
        (
            shape((rows, depth), f32),
            shape((rows + tail, depth), bf16),
            shape((area, width), f32),
            shape((3 * held, width), bf16),
            shape(couple_features.shape, f32),
            shape((area, width), bf16),
        ),
        [pltpu.VMEM(x.shape, x.dtype) for x in args]
        + [pltpu.SemaphoreType.DMA((len(args),)), pltpu.VMEM((tail, depth), f32)],
        smem=1,
        hbm=True,
    )(amino_present, *args)
    pending = ()
    if halves:
        row_blocks, row_relative = gather(payload, "res")
        turned, crossed = turn_pairs(couple_features)
        flat = shape((area, width), bf16)
        came, given, terms = call(turn_kernel, (flat, flat, shape((6 * held, width), bf16)))(
            turned, trimul_entry_matrix, couple_logit_matrix.T, terms
        )
        passed = flip(given, "aux")
        other_left, other_came = flip(left, "br"), flip(came, "br")
        cube = shape(couple_features.shape, f32)
        scratch = [pltpu.VMEM(couple_features.shape, f32)]
        far = call(far_kernel, cube, smem=1)(*presence, turned, crossed, trimul_entry_matrix)
        nearest = lax.optimization_barrier((near, far))[0]
        early = lambda other_half, right: call(
            functools.partial(early_kernel, other_half), cube, scratch
        )(left, came, other_left, other_came, right)
        sent = early(True, nearest)
        ready = lax.optimization_barrier((passed, far, sent, row_blocks[2], row_blocks[3], row_blocks[1]))[0]
        other_passed = flip(ready, "br")
        operands = (came, passed, other_came, other_passed, far)
        terms, side_relative = (terms, flip(terms, "br"), passed, other_passed), True
        places = [(0, 0, None), (0, 3 * held, 2), (1, 0, None), (1, 3 * held, 3)]
        late = lambda other_half, kind, sums, after: call(
            functools.partial(late_kernel, other_half),
            shape(couple_features.shape, kind),
            scratch,
            after=after,
        )(*operands, sums)
        sent = late(True, bf16, sent, ())
        received = flip(sent, "res", 2)
        pending = (sent,)
    else:
        row_blocks, row_relative = gather(payload, "res")
        terms, side_relative = gather_side(terms)
        places = [(index, 0, None) for index in range(side)]

    after, payload = call(
        functools.partial(row_kernel, row_relative, side_relative, places, lines, positions),
        (shape((rows, depth), f32), shape((rows + tail, depth), bf16)),
        [
            pltpu.VMEM((pair_rows * heads, residues), f32),
            pltpu.VMEM((lines, residues, depth), bf16),
            pltpu.VMEM((lines, residues, depth), bf16),
            pltpu.VMEM((rows, depth), bf16),
        ],
        after=pending,
    )(*terms, *row_blocks, payload, embedded, horizontal_entry_matrix, horizontal_exit_matrix)
    if halves:
        kept = early(False, lax.optimization_barrier((near, payload))[0])
        column_blocks = double_side(payload, (kept,))
        kept = late(False, f32, kept, ())
        pending = (kept,)
    else:
        column_blocks = gather_side(payload)[0]
    group = 8
    alignment_output = call(
        functools.partial(column_kernel, lines, positions, group, heads),
        shape((lines, positions, depth), bf16),
        [
            pltpu.VMEM((side * lines, positions, depth), f32),
            pltpu.VMEM((side * lines, positions, depth), f32),
            pltpu.VMEM((lines, positions, depth), f32),
        ],
        after=pending,
    )(
        *column_blocks,
        payload,
        after,
        vertical_entry_matrix,
        vertical_exit_matrix,
        feedforward_first_matrix,
        feedforward_second_matrix,
    )
    if halves:
        pair_output = call(
            finish_kernel,
            shape(couple_features.shape, bf16),
            [pltpu.VMEM(couple_features.shape, f32)],
            smem=1,
        )(amino_present, kept, couple_features, gate, trimul_exit_matrix, received)
    else:
        pair_output = triangle_by_gather(
            couple_features, presence, trimul_entry_matrix, trimul_exit_matrix, gate
        )
    return (alignment_output, pair_output)


def solution(mesh):
    return jax.shard_map(
        on_device,
        mesh=mesh,
        in_specs=(
            P(("grp", "br", "aux"), "res", None),
            P(("grp", "res"), ("br", "aux"), None),
            P(("grp", "br", "aux"), "res"),
            P(("grp", "br", "aux"), "res"),
            P("grp"),
            P(),
            P(),
            P(),
            P(),
            P(),
            P(),
            P(),
            P(),
            P(),
            P(),
        ),
        out_specs=(P(("grp", "br", "aux"), "res", None), P(("grp", "res"), ("br", "aux"), None)),
        check_vma=False,
    )
```

```python
import functools

import jax
import jax.numpy as jnp
from jax import lax
from jax.experimental import pallas as pl
from jax.experimental.pallas import tpu as pltpu
from jax.sharding import PartitionSpec as P

epsilon = 1e-05
masked_fill_value = 1000000000.0
bf16 = jnp.bfloat16
f32 = jnp.float32
SIDE = ("br", "aux")
ALL = ("res", "br", "aux")
NT = (((1,), (1,)), ((), ()))
TN = (((0,), (0,)), ((), ()))


def normalize(values):
    average = jnp.mean(values, axis=-1, keepdims=True)
    centred = values - average
    variance = jnp.mean(centred * centred, axis=-1, keepdims=True)
    return centred * lax.rsqrt(variance + epsilon)


def sigmoid(values):
    return 1.0 / (1.0 + jnp.exp(-values))


def dot(left, right):
    return jnp.dot(left, right, preferred_element_type=f32)


def iota(shape, dim):
    return lax.broadcasted_iota(jnp.int32, shape, dim)


def round_up(count, step):
    return -(-count // step) * step


def side_index():
    return lax.axis_index("br") * lax.axis_size("aux") + lax.axis_index("aux")


def embed_kernel(features, ids, present, table, embedded, payload, tail):
    lines, positions, depth = features.shape
    kinds = table.shape[0]
    rows = lines * positions
    for line in range(lines):
        onehot = (iota((kinds, positions), 0) == ids[line : line + 1, :]).astype(bf16)
        token = lax.dot_general(onehot, table[...], TN, preferred_element_type=f32)
        values = features[line].astype(f32) + token
        span = slice(line * positions, (line + 1) * positions)
        embedded[span, :] = values
        payload[span, :] = normalize(values).astype(bf16)
    tail[...] = jnp.zeros_like(tail)
    tail[:lines, :positions] = present[...].astype(f32)
    payload[rows:, :] = tail[...].astype(bf16)


def attend(queries, keys, values, bias, heads):
    count, depth = queries.shape
    width = depth // heads
    own = (iota((heads, depth), 1) // width == iota((heads, depth), 0)).astype(f32)
    spread = (queries[:, None, :] * own[None]).reshape(count * heads, depth).astype(bf16)
    scores = lax.dot_general(spread, keys, NT, preferred_element_type=f32) * width ** (-0.5)
    scores = bias(scores)
    powers = jnp.exp(scores - jnp.max(scores, axis=-1, keepdims=True))
    weights = (powers * (1.0 / jnp.sum(powers, axis=-1, keepdims=True))).astype(bf16)
    mixed = dot(weights, values).reshape(count, heads, depth)
    return jnp.sum(mixed * own[None], axis=1)


def row_kernel(relative, side_relative, places, lines, positions, *refs):
    used = 1 + max(max(index, index if other is None else other) for index, _, other in places)
    terms, refs = refs[:used], refs[used:]
    blocks = refs[: len(refs) - 10]
    own, embedded, entry, leave, after, payload, bias, keys, values, mix = refs[len(refs) - 10 :]
    depth = leave.shape[0]
    heads = bias.shape[0] // positions
    rows = lines * positions
    key_count = bias.shape[1]
    me = lax.axis_index("res")
    lanes = terms[0].shape[1]
    per = lanes // positions
    side = side_index()
    sums = []
    held = positions * heads // per
    sums = []
    for source, start, other in places:
        parts = []
        for index in range(3):
            first = index * held
            part = terms[source][start + first : start + first + held, :].astype(f32)
            if other is not None:
                choice = terms[other][first : first + held, :].astype(f32)
                part = jnp.where(on_turn(), choice, part)
            parts.append(part)
        sums.append(parts[0] + parts[1] + parts[2])
    place = iota((heads, key_count), 1) // positions
    for line in range(positions):
        total = jnp.zeros((heads, key_count), f32)
        for slot, values_of in enumerate(sums):
            source = (side ^ slot) if side_relative else slot
            part = values_of[(line // per) * heads : (line // per + 1) * heads]
            part = pltpu.roll(part, ((source - line % per + lanes) % per) * positions, 1)
            part = jnp.concatenate([part] * (key_count // lanes), axis=1)
            total = jnp.where(place == source, part, total)
        bias[line * heads : (line + 1) * heads, :] = total
    penalty = jnp.zeros((payload.shape[0] - rows, key_count), f32)
    for slot, block in enumerate(blocks):
        source = (me ^ slot) if relative else slot
        place = iota((depth, key_count), 0)
        place = (place < positions) & (iota((depth, key_count), 1) == place + source * positions)
        penalty += dot(block[rows:, :], place.astype(bf16))
        projected = dot(block[:rows, :], entry[:, depth : 3 * depth]).astype(bf16)
        for line in range(lines):
            span = pl.ds(pl.multiple_of(source * positions, positions), positions)
            part = projected[line * positions : (line + 1) * positions]
            keys[line, span, :] = part[:, :depth]
            values[line, span, :] = part[:, depth:]
    penalty = masked_fill_value * (penalty - 1.0)
    normed = own[:rows, :]
    queries = dot(normed, entry[:, :depth]).astype(bf16).astype(f32)
    gate = sigmoid(dot(normed, entry[:, 3 * depth :]))
    for line in range(lines):
        span = slice(line * positions, (line + 1) * positions)
        fixed = lambda scores, line=line: scores + bias[...] + penalty[line : line + 1, :]
        mixed = attend(queries[span], keys[line], values[line], fixed, heads)
        mix[span, :] = (gate[span] * mixed).astype(bf16)
    result = embedded[...] + dot(mix[...], leave[...])
    after[...] = result
    payload[:rows, :] = normalize(result).astype(bf16)
    payload[rows:, :] = own[rows:, :]


def column_kernel(lines, positions, group, heads, *refs):
    blocks = refs[: len(refs) - 10]
    own, after, entry, leave, first, second, output, keys, values, mix = refs[len(refs) - 10 :]
    depth = leave.shape[0]
    rows = lines * positions
    presence = []
    blocks = [
        block.at[part] if len(block.shape) == 3 else block
        for block in blocks
        for part in range(block.shape[0] if len(block.shape) == 3 else 1)
    ]
    for slot, block in enumerate(blocks):
        projected = dot(block[:rows, :], entry[:, depth : 3 * depth])
        span = slice(slot * lines, (slot + 1) * lines)
        keys[span] = projected[:, :depth].reshape(lines, positions, depth)
        values[span] = projected[:, depth:].reshape(lines, positions, depth)
        presence.append(block[rows:, :])
    tail = presence[0].shape[0]
    presence = jnp.concatenate(presence, axis=0)
    normed = own[:rows, :]
    queries = dot(normed, entry[:, :depth]).astype(bf16).astype(f32)
    queries = queries.reshape(lines, positions, depth)
    gate = sigmoid(dot(normed, entry[:, 3 * depth :])).reshape(lines, positions, depth)
    key_count = len(blocks) * lines * group
    row = iota((presence.shape[0], key_count), 0)
    lane = iota((presence.shape[0], key_count), 1)
    chosen = (row % tail < lines) & ((row // tail) * lines + row % tail == lane // group)
    shape = (lines * group * heads, key_count)
    same = (iota(shape, 0) // heads) % group == iota(shape, 1) % group
    for start in range(0, positions, group):
        span = slice(start, start + group)
        pick = (iota((depth, key_count), 0) == start + iota((depth, key_count), 1) % group)
        held = dot(presence, pick.astype(bf16))
        held = jnp.sum(jnp.where(chosen, held, 0.0), axis=0, keepdims=True)
        penalty = masked_fill_value * (held - 1.0)
        fixed = lambda scores: jnp.where(same, scores + penalty, -jnp.inf)
        mixed = attend(
            queries[:, span].reshape(lines * group, depth),
            keys[:, span].reshape(key_count, depth).astype(bf16),
            values[:, span].reshape(key_count, depth).astype(bf16),
            fixed,
            heads,
        )
        mix[:, span] = gate[:, span] * mixed.reshape(lines, group, depth)
    mixed = mix[...].reshape(rows, depth).astype(bf16)
    result = after[...] + dot(mixed, leave[...])
    hidden = jnp.maximum(dot(normalize(result).astype(bf16), first[...]), 0.0).astype(bf16)
    result = result + dot(hidden, second[...])
    output[...] = result.astype(bf16).reshape(output.shape)


def fetch(sources, buffers, semaphores):
    copies = [
        pltpu.make_async_copy(source, buffer, semaphores.at[index])
        for index, (source, buffer) in enumerate(zip(sources, buffers))
    ]
    for copy in copies:
        copy.start()
    for copy in copies:
        copy.wait()


def split(values):
    high = values.astype(bf16)
    rest = values - high.astype(f32)
    middle = rest.astype(bf16)
    return high, middle, (rest - middle.astype(f32)).astype(bf16)


def store_terms(logit, out, start):
    heads, count = logit.shape
    lanes = out.shape[1]
    for index, term in enumerate(split(logit)):
        for part in range(count // lanes):
            base = start + (index * (count // lanes) + part) * heads
            out[base : base + heads, :] = term[:, part * lanes : (part + 1) * lanes]


def first_kernel(count, *refs):
    sources, outputs, rest = refs[:count], refs[count : count + 3], refs[count + 3 :]
    buffers, semaphores, tail = rest[:count], rest[count], rest[count + 1]
    fetch(sources, buffers, semaphores)
    embedded, payload, terms = outputs
    embed_kernel(*buffers[:4], embedded, payload, tail)
    pairs, logits = buffers[4:]
    lines, positions, width = pairs.shape
    normed = normalize(pairs[...].astype(f32).reshape(lines * positions, width)).astype(bf16)
    logit = lax.dot_general(logits[...], normed, NT, preferred_element_type=f32)
    store_terms(logit, terms, 0)


def pair_kernel(present, present_row, pairs, entry, gate, near, left):
    lines, positions, width = pairs.shape
    normed = normalize(pairs[...].astype(f32).reshape(lines * positions, width)).astype(bf16)
    projected = dot(normed, entry[...])
    gate[...] = sigmoid(projected[:, 4 * width :])
    left[...] = (sigmoid(projected[:, width : 2 * width]) * projected[:, :width]).astype(bf16)
    operand = sigmoid(projected[:, 3 * width : 4 * width]) * projected[:, 2 * width : 3 * width]
    mask_right(lax.axis_index("res"), operand.astype(bf16), present, present_row, near)


def on_turn():
    return lax.axis_index("res") % 2 == lax.axis_index("aux")


def hold_kernel(terms, present_row, out):
    out[...] = terms[...]


def turn_kernel(pairs, entry, logits, terms, came, given, both):
    lines, positions, width = pairs.shape
    held = terms.shape[0]
    normed = normalize(pairs[...].astype(f32).reshape(lines * positions, width)).astype(bf16)
    projected = dot(normed, entry[:, : 2 * width])
    operand = (sigmoid(projected[:, width:]) * projected[:, :width]).astype(bf16)
    came[...] = operand
    given[...] = operand

    @pl.when(jnp.logical_not(on_turn()))
    def _():
        given[:held, :] = terms[...]

    both[:held, :] = terms[...]
    logit = lax.dot_general(logits[...], normed, NT, preferred_element_type=f32)
    store_terms(logit, both, held)


def gated(pairs, weight):
    lines, positions, width = pairs.shape
    normed = normalize(pairs[...].astype(f32).reshape(lines * positions, width)).astype(bf16)
    projected = dot(normed, weight)
    return (sigmoid(projected[:, width:]) * projected[:, :width]).astype(bf16)


def left_kernel(pairs, entry, left):
    width = pairs.shape[2]
    left[...] = gated(pairs, entry[:, : 2 * width])


def mask_right(source, operand, present, present_row, right):
    lines, positions, width = right.shape
    lane = iota((positions, present_row.shape[1]), 1)
    lane = lane == iota((positions, present_row.shape[1]), 0) + side_index() * positions
    valid = jnp.where(lane, present_row[...].astype(f32), 0.0)
    valid = jnp.sum(valid, axis=1, keepdims=True)
    operand = operand.astype(f32)
    for line in range(lines):
        both = valid * present[source * lines + line].astype(f32)
        right[line] = (operand[line * positions : (line + 1) * positions] * both).astype(
            right.dtype
        )


def right_operand(relative, slot, present, present_row, pairs, entry, right):
    width = pairs.shape[2]
    source = (lax.axis_index("res") ^ slot) if relative else slot
    operand = gated(pairs, entry[:, 2 * width : 4 * width])
    mask_right(source, operand, present, present_row, right)


def pick_left(relative, slot, lefts, left):
    source = (lax.axis_index("res") ^ slot) if relative[0] else slot
    side = side_index()
    for place, block in enumerate(lefts):
        held = (side ^ place) if relative[1] else place

        @pl.when(held == source)
        def _():
            left[...] = block[...].astype(f32).reshape(left.shape)


def accumulate(left, right, total_in, total):
    step = 4
    depth, positions, width = right.shape

    def body(index, carry):
        base = index * step
        sums = [None if total_in is None else total_in[base + t] for t in range(step)]
        for line in range(depth):
            line_right = right[line].astype(f32)
            for t in range(step):
                term = left[line, pl.ds(base + t, 1), :] * line_right
                sums[t] = term if sums[t] is None else sums[t] + term
        for t in range(step):
            total[base + t] = sums[t]
        return carry

    lax.fori_loop(0, total.shape[0] // step, body, 0)


def middle_kernel(relative, slots, *refs):
    rights, lefts = refs[: len(slots)], refs[len(slots) : -2]
    total, left = refs[-2:]
    for index, slot in enumerate(slots):
        pick_left(relative, slot, lefts, left)
        accumulate(left, rights[index], total if index else None, total)


def last_kernel(relative, slot, *refs):
    present, present_row, pairs, entry, total_in, own, gate, leave = refs[:8]
    lefts, (out, left, right, total) = refs[8:-4], refs[-4:]
    lines, positions, width = out.shape
    pick_left(relative, slot, lefts, left)
    right_operand(relative[0], slot, present, present_row, pairs, entry, right)
    accumulate(left, right, total_in, total)
    me = lax.axis_index("res")
    for line in range(lines):
        total[line] = total[line] * present[me * lines + line].astype(f32)
    product = total[...].reshape(lines * positions, width).astype(bf16).astype(f32)
    update = gate[...] * dot(normalize(product).astype(bf16), leave[...])
    out[...] = (own[...].astype(f32) + update.reshape(out.shape)).astype(bf16)


def far_kernel(present, present_row, turned, crossed, entry, right):
    width = turned.shape[2]
    pairs = jnp.where(on_turn(), turned[...].astype(f32), crossed[...].astype(f32))
    operand = gated(pairs, entry[:, 2 * width : 4 * width])
    mask_right(lax.axis_index("res") ^ 1, operand, present, present_row, right)


def accumulate_rows(left, right, total_in, total):
    step = 8

    def body(index, carry):
        base = index * step
        sums = [None if total_in is None else total_in[base + t] for t in range(step)]
        for line in range(right.shape[0]):
            line_right = right[line]
            for t in range(step):
                term = left[line, pl.ds(base + t, 1), :] * line_right
                sums[t] = term if sums[t] is None else sums[t] + term
        for t in range(step):
            total[base + t] = sums[t].astype(total.dtype)
        return carry

    lax.fori_loop(0, total.shape[0] // step, body, 0)


def load_left(block, base, left):
    lines, count, _ = left.shape
    for line in range(lines):
        start = base + line * count
        left[line] = block[start : start + count, :].astype(f32)


def early_kernel(other_half, own, came, other_own, other_came, near, sums, left):
    same = lax.axis_index("br") == lax.axis_index("res") // 2
    mine = jnp.logical_not(same) if other_half else same
    turn = on_turn()
    other, straight = jnp.logical_not(mine), jnp.logical_not(turn)
    pl.when(mine & turn)(lambda: load_left(own, 0, left))
    pl.when(mine & straight)(lambda: load_left(came, 0, left))
    pl.when(other & turn)(lambda: load_left(other_own, 0, left))
    pl.when(other & straight)(lambda: load_left(other_came, 0, left))
    accumulate_rows(left, near, None, sums)


def late_kernel(other_half, came, passed, other_came, other_passed, far, sums, total, left):
    same = lax.axis_index("br") == lax.axis_index("res") // 2
    mine = jnp.logical_not(same) if other_half else same
    turn = on_turn()
    other, straight = jnp.logical_not(mine), jnp.logical_not(turn)
    pl.when(mine & turn)(lambda: load_left(came, 0, left))
    pl.when(mine & straight)(lambda: load_left(passed, 0, left))
    pl.when(other & turn)(lambda: load_left(other_came, 0, left))
    pl.when(other & straight)(lambda: load_left(other_passed, 0, left))
    accumulate_rows(left, far, sums, total)


def finish_kernel(present, kept, own, gate, leave, *refs):
    received, (out, total) = refs[:-2], refs[-2:]
    lines, positions, width = out.shape
    me = lax.axis_index("res")
    each = lines // len(received)
    for line in range(lines):
        sums = kept[line] + received[line // each][line % each].astype(f32)
        total[line] = sums * present[me * lines + line].astype(f32)
    product = total[...].reshape(lines * positions, width).astype(bf16).astype(f32)
    update = gate[...] * dot(normalize(product).astype(bf16), leave[...])
    out[...] = (own[...].astype(f32) + update.reshape(out.shape)).astype(bf16)


def gather(block, axis):
    size = lax.axis_size(axis)
    if size in (1, 2, 4):
        return [block] + [flip(block, axis, d) for d in range(1, size)], True
    whole = lax.all_gather(block, axis)
    return [whole[i] for i in range(size)], False


def flip(block, axis, bit=1):
    return lax.ppermute(block, axis, [(i, i ^ bit) for i in range(lax.axis_size(axis))])


def gather_side(block):
    if lax.axis_size("br") == 2 and lax.axis_size("aux") == 2:
        near = flip(block, "br")
        far = flip(block, "aux")
        return [block, far, near, flip(far, "br")], True
    whole = lax.all_gather(block, SIDE)
    return [whole[i] for i in range(whole.shape[0])], False


def pair_up(block, other, out):
    out[0] = block[...]
    out[1] = other[...]


def double(block, axis, bit, axis_after, ahead):
    far = flip(block, axis, bit)
    pair = call(pair_up, shape((2, *block.shape), block.dtype), after=ahead)(block, far)
    return [pair, flip(pair, axis_after)]


def double_side(block, ahead):
    return double(block, "aux", 1, "br", ahead)


def shape(dims, kind):
    return jax.ShapeDtypeStruct(dims, kind)


def call(kernel, out_shape, scratch=(), smem=0, after=(), hbm=False):
    def run(*args):
        count, unread = len(args), len(after)

        def ordered(*refs):
            kernel(*refs[:count], *refs[count + unread :])

        return pl.pallas_call(
            ordered,
            out_shape=out_shape,
            in_specs=[pl.BlockSpec(memory_space=pltpu.SMEM)] * smem
            + [pl.BlockSpec(memory_space=pltpu.HBM if hbm else pltpu.VMEM)] * (count - smem)
            + [pl.BlockSpec(memory_space=pl.ANY)] * unread,
            out_specs=jax.tree.map(lambda _: pl.BlockSpec(memory_space=pltpu.VMEM), out_shape),
            scratch_shapes=list(scratch),
            compiler_params=pltpu.CompilerParams(vmem_limit_bytes=(62 if hbm else 48) * 1024 * 1024),
            cost_estimate=pl.CostEstimate(flops=1, bytes_accessed=1, transcendentals=0),
        )(*args, *after)

    return run


def triangle_by_gather(pairs, presence, entry, leave, gate):
    res = lax.axis_size("res")
    side = lax.axis_size("br") * lax.axis_size("aux")
    rows, cols, width = pairs.shape
    cube = pltpu.VMEM((rows, cols, width), f32)
    turned = lax.ppermute(
        pairs, ALL, [(r * side + b, b * side + r) for r in range(res) for b in range(side)]
    )
    left = call(left_kernel, shape((rows * cols, width), bf16))(turned, entry)
    lefts, left_relative = gather_side(left)
    blocks, pair_relative = gather(pairs, "res")
    relative = (pair_relative, left_relative)
    slots = list(range(res - 1))
    rights = [
        call(
            functools.partial(right_operand, pair_relative, slot), shape(pairs.shape, bf16), smem=1
        )(*presence, blocks[slot], entry)
        for slot in slots
    ]
    total = call(
        functools.partial(middle_kernel, relative, slots), shape(pairs.shape, f32), [cube]
    )(*rights, *lefts)
    return call(
        functools.partial(last_kernel, relative, res - 1),
        shape(pairs.shape, bf16),
        [cube, cube, cube],
        smem=1,
    )(*presence, blocks[-1], entry, total, pairs, gate, leave, *lefts)


def turn_pairs(pairs):
    index = lambda half, low, br, aux: ((half * 2 + low) * 2 + br) * 2 + aux
    every = [(h, low, br, aux) for h in (0, 1) for low in (0, 1) for br in (0, 1) for aux in (0, 1)]
    goes = lambda h, l, br, a: index(h, l, br, 1 - a) if a == l else index(h, 1 - l, br, a)
    turned = lax.ppermute(pairs, ALL, [(index(*place), goes(*place)) for place in every])
    crossed = lax.ppermute(
        pairs, ALL, [(index(h, l, br, a), index(h, 1 - l, br, a)) for h, l, br, a in every if a == l]
    )
    return turned, crossed


def on_device(
    homolog_features,
    couple_features,
    symbol_ids,
    entry_present,
    amino_present,
    symbol_lookup_matrix,
    horizontal_entry_matrix,
    couple_logit_matrix,
    horizontal_exit_matrix,
    vertical_entry_matrix,
    vertical_exit_matrix,
    feedforward_first_matrix,
    feedforward_second_matrix,
    trimul_entry_matrix,
    trimul_exit_matrix,
):
    lines, positions, depth = homolog_features.shape
    pair_rows, pair_cols, width = couple_features.shape
    heads = couple_logit_matrix.shape[1]
    res = lax.axis_size("res")
    side = lax.axis_size("br") * lax.axis_size("aux")
    rows = lines * positions
    tail = round_up(lines, 16)
    residues = positions * res
    area = pair_rows * pair_cols
    held = pair_rows * pair_cols * heads // width
    presence = [amino_present, amino_present[None, :]]
    halves = (res, lax.axis_size("br"), lax.axis_size("aux")) == (4, 2, 2)

    args = (
        homolog_features,
        symbol_ids,
        entry_present,
        symbol_lookup_matrix,
        couple_features,
        couple_logit_matrix.T,
    )
    embedded, payload, terms = call(
        functools.partial(first_kernel, len(args)),
        (
            shape((rows, depth), f32),
            shape((rows + tail, depth), bf16),
            shape((3 * held, width), bf16),
        ),
        [pltpu.VMEM(x.shape, x.dtype) for x in args]
        + [pltpu.SemaphoreType.DMA((len(args),)), pltpu.VMEM((tail, depth), f32)],
        hbm=True,
    )(*args)
    flat = shape((area, width), bf16)
    of_pairs = lambda pairs: call(
        pair_kernel, (shape((area, width), f32), shape(pairs.shape, f32), flat), smem=1
    )(*presence, pairs, trimul_entry_matrix)
    pending = ()
    if halves:
        row_blocks, row_relative = gather(payload, "res")
        turned, crossed = turn_pairs(couple_features)
        terms = call(hold_kernel, shape(terms.shape, bf16))(terms, presence[1])
        came, given, terms = call(turn_kernel, (flat, flat, shape((6 * held, width), bf16)))(
            turned, trimul_entry_matrix, couple_logit_matrix.T, terms
        )
        passed = flip(given, "aux")
        gate, near, left = of_pairs(lax.optimization_barrier((couple_features, came))[0])
        other_left, other_came = flip(left, "br"), flip(came, "br")
        cube = shape(couple_features.shape, f32)
        scratch = [pltpu.VMEM(couple_features.shape, f32)]
        far = call(far_kernel, cube, smem=1)(*presence, turned, crossed, trimul_entry_matrix)
        ready = lax.optimization_barrier((passed, far, row_blocks[2], row_blocks[3], row_blocks[1]))[0]
        other_passed = flip(ready, "br")
        nearest = lax.optimization_barrier((near, passed, far))[0]
        early = lambda other_half, right: call(
            functools.partial(early_kernel, other_half), cube, scratch
        )(left, came, other_left, other_came, right)
        sent = early(True, nearest)
        operands = (came, passed, other_came, other_passed, far)
        terms, side_relative = (terms, flip(terms, "br"), passed, other_passed), True
        places = [(0, 0, None), (0, 3 * held, 2), (1, 0, None), (1, 3 * held, 3)]
        late = lambda other_half, kind, sums, after: call(
            functools.partial(late_kernel, other_half),
            shape(couple_features.shape, kind),
            scratch,
            after=after,
        )(*operands, sums)
        sent = late(True, bf16, sent, ())
        received = flip(sent, "res", 2)
        pending = (sent,)
    else:
        row_blocks, row_relative = gather(payload, "res")
        gate = of_pairs(couple_features)[0]
        terms, side_relative = gather_side(terms)
        places = [(index, 0, None) for index in range(side)]

    after, payload = call(
        functools.partial(row_kernel, row_relative, side_relative, places, lines, positions),
        (shape((rows, depth), f32), shape((rows + tail, depth), bf16)),
        [
            pltpu.VMEM((pair_rows * heads, residues), f32),
            pltpu.VMEM((lines, residues, depth), bf16),
            pltpu.VMEM((lines, residues, depth), bf16),
            pltpu.VMEM((rows, depth), bf16),
        ],
        after=pending,
    )(*terms, *row_blocks, payload, embedded, horizontal_entry_matrix, horizontal_exit_matrix)
    if halves:
        kept = early(False, lax.optimization_barrier((near, payload))[0])
        column_blocks = double_side(payload, (kept,))
        kept = late(False, f32, kept, ())
        pending = (kept,)
    else:
        column_blocks = gather_side(payload)[0]
    group = 8
    alignment_output = call(
        functools.partial(column_kernel, lines, positions, group, heads),
        shape((lines, positions, depth), bf16),
        [
            pltpu.VMEM((side * lines, positions, depth), f32),
            pltpu.VMEM((side * lines, positions, depth), f32),
            pltpu.VMEM((lines, positions, depth), f32),
        ],
        after=pending,
    )(
        *column_blocks,
        payload,
        after,
        vertical_entry_matrix,
        vertical_exit_matrix,
        feedforward_first_matrix,
        feedforward_second_matrix,
    )
    if halves:
        pair_output = call(
            finish_kernel,
            shape(couple_features.shape, bf16),
            [pltpu.VMEM(couple_features.shape, f32)],
            smem=1,
        )(amino_present, kept, couple_features, gate, trimul_exit_matrix, received)
    else:
        pair_output = triangle_by_gather(
            couple_features, presence, trimul_entry_matrix, trimul_exit_matrix, gate
        )
    return (alignment_output, pair_output)


def solution(mesh):
    return jax.shard_map(
        on_device,
        mesh=mesh,
        in_specs=(
            P(("grp", "br", "aux"), "res", None),
            P(("grp", "res"), ("br", "aux"), None),
            P(("grp", "br", "aux"), "res"),
            P(("grp", "br", "aux"), "res"),
            P("grp"),
            P(),
            P(),
            P(),
            P(),
            P(),
            P(),
            P(),
            P(),
            P(),
            P(),
        ),
        out_specs=(P(("grp", "br", "aux"), "res", None), P(("grp", "res"), ("br", "aux"), None)),
        check_vma=False,
    )
```

```python
import functools

import jax
import jax.numpy as jnp
from jax import lax
from jax.experimental import pallas as pl
from jax.experimental.pallas import tpu as pltpu
from jax.sharding import PartitionSpec as P

epsilon = 1e-05
masked_fill_value = 1000000000.0
bf16 = jnp.bfloat16
f32 = jnp.float32
SIDE = ("br", "aux")
ALL = ("res", "br", "aux")
NT = (((1,), (1,)), ((), ()))
TN = (((0,), (0,)), ((), ()))


def normalize(values):
    average = jnp.mean(values, axis=-1, keepdims=True)
    centred = values - average
    variance = jnp.mean(centred * centred, axis=-1, keepdims=True)
    return centred * lax.rsqrt(variance + epsilon)


def sigmoid(values):
    return 1.0 / (1.0 + jnp.exp(-values))


def dot(left, right):
    return jnp.dot(left, right, preferred_element_type=f32)


def iota(shape, dim):
    return lax.broadcasted_iota(jnp.int32, shape, dim)


def round_up(count, step):
    return -(-count // step) * step


def side_index():
    return lax.axis_index("br") * lax.axis_size("aux") + lax.axis_index("aux")


def embed_kernel(features, ids, present, table, embedded, payload, tail):
    lines, positions, depth = features.shape
    kinds = table.shape[0]
    rows = lines * positions
    for line in range(lines):
        onehot = (iota((kinds, positions), 0) == ids[line : line + 1, :]).astype(bf16)
        token = lax.dot_general(onehot, table[...], TN, preferred_element_type=f32)
        values = features[line].astype(f32) + token
        span = slice(line * positions, (line + 1) * positions)
        embedded[span, :] = values
        payload[span, :] = normalize(values).astype(bf16)
    tail[...] = jnp.zeros_like(tail)
    tail[:lines, :positions] = present[...].astype(f32)
    payload[rows:, :] = tail[...].astype(bf16)


def attend(queries, keys, values, bias, heads):
    count, depth = queries.shape
    width = depth // heads
    own = (iota((heads, depth), 1) // width == iota((heads, depth), 0)).astype(f32)
    spread = (queries[:, None, :] * own[None]).reshape(count * heads, depth).astype(bf16)
    scores = lax.dot_general(spread, keys, NT, preferred_element_type=f32) * width ** (-0.5)
    scores = bias(scores)
    powers = jnp.exp(scores - jnp.max(scores, axis=-1, keepdims=True))
    weights = (powers * (1.0 / jnp.sum(powers, axis=-1, keepdims=True))).astype(bf16)
    mixed = dot(weights, values).reshape(count, heads, depth)
    return jnp.sum(mixed * own[None], axis=1)


def row_kernel(relative, side_relative, places, lines, positions, *refs):
    used = 1 + max(max(index, index if other is None else other) for index, _, other in places)
    terms, refs = refs[:used], refs[used:]
    blocks = refs[: len(refs) - 10]
    own, embedded, entry, leave, after, payload, bias, keys, values, mix = refs[len(refs) - 10 :]
    depth = leave.shape[0]
    heads = bias.shape[0] // positions
    rows = lines * positions
    key_count = bias.shape[1]
    me = lax.axis_index("res")
    lanes = terms[0].shape[1]
    per = lanes // positions
    side = side_index()
    sums = []
    held = positions * heads // per
    sums = []
    for source, start, other in places:
        parts = []
        for index in range(3):
            first = index * held
            part = terms[source][start + first : start + first + held, :].astype(f32)
            if other is not None:
                choice = terms[other][first : first + held, :].astype(f32)
                part = jnp.where(on_turn(), choice, part)
            parts.append(part)
        sums.append(parts[0] + parts[1] + parts[2])
    place = iota((heads, key_count), 1) // positions
    for line in range(positions):
        total = jnp.zeros((heads, key_count), f32)
        for slot, values_of in enumerate(sums):
            source = (side ^ slot) if side_relative else slot
            part = values_of[(line // per) * heads : (line // per + 1) * heads]
            part = pltpu.roll(part, ((source - line % per + lanes) % per) * positions, 1)
            part = jnp.concatenate([part] * (key_count // lanes), axis=1)
            total = jnp.where(place == source, part, total)
        bias[line * heads : (line + 1) * heads, :] = total
    penalty = jnp.zeros((payload.shape[0] - rows, key_count), f32)
    for slot, block in enumerate(blocks):
        source = (me ^ slot) if relative else slot
        place = iota((depth, key_count), 0)
        place = (place < positions) & (iota((depth, key_count), 1) == place + source * positions)
        penalty += dot(block[rows:, :], place.astype(bf16))
        projected = dot(block[:rows, :], entry[:, depth : 3 * depth]).astype(bf16)
        for line in range(lines):
            span = pl.ds(pl.multiple_of(source * positions, positions), positions)
            part = projected[line * positions : (line + 1) * positions]
            keys[line, span, :] = part[:, :depth]
            values[line, span, :] = part[:, depth:]
    penalty = masked_fill_value * (penalty - 1.0)
    normed = own[:rows, :]
    queries = dot(normed, entry[:, :depth]).astype(bf16).astype(f32)
    gate = sigmoid(dot(normed, entry[:, 3 * depth :]))
    for line in range(lines):
        span = slice(line * positions, (line + 1) * positions)
        fixed = lambda scores, line=line: scores + bias[...] + penalty[line : line + 1, :]
        mixed = attend(queries[span], keys[line], values[line], fixed, heads)
        mix[span, :] = (gate[span] * mixed).astype(bf16)
    result = embedded[...] + dot(mix[...], leave[...])
    after[...] = result
    payload[:rows, :] = normalize(result).astype(bf16)
    payload[rows:, :] = own[rows:, :]


def column_kernel(lines, positions, group, heads, *refs):
    blocks = refs[: len(refs) - 10]
    own, after, entry, leave, first, second, output, keys, values, mix = refs[len(refs) - 10 :]
    depth = leave.shape[0]
    rows = lines * positions
    presence = []
    blocks = [
        block.at[part] if len(block.shape) == 3 else block
        for block in blocks
        for part in range(block.shape[0] if len(block.shape) == 3 else 1)
    ]
    for slot, block in enumerate(blocks):
        projected = dot(block[:rows, :], entry[:, depth : 3 * depth])
        span = slice(slot * lines, (slot + 1) * lines)
        keys[span] = projected[:, :depth].reshape(lines, positions, depth)
        values[span] = projected[:, depth:].reshape(lines, positions, depth)
        presence.append(block[rows:, :])
    tail = presence[0].shape[0]
    presence = jnp.concatenate(presence, axis=0)
    normed = own[:rows, :]
    queries = dot(normed, entry[:, :depth]).astype(bf16).astype(f32)
    queries = queries.reshape(lines, positions, depth)
    gate = sigmoid(dot(normed, entry[:, 3 * depth :])).reshape(lines, positions, depth)
    key_count = len(blocks) * lines * group
    row = iota((presence.shape[0], key_count), 0)
    lane = iota((presence.shape[0], key_count), 1)
    chosen = (row % tail < lines) & ((row // tail) * lines + row % tail == lane // group)
    shape = (lines * group * heads, key_count)
    same = (iota(shape, 0) // heads) % group == iota(shape, 1) % group
    for start in range(0, positions, group):
        span = slice(start, start + group)
        pick = (iota((depth, key_count), 0) == start + iota((depth, key_count), 1) % group)
        held = dot(presence, pick.astype(bf16))
        held = jnp.sum(jnp.where(chosen, held, 0.0), axis=0, keepdims=True)
        penalty = masked_fill_value * (held - 1.0)
        fixed = lambda scores: jnp.where(same, scores + penalty, -jnp.inf)
        mixed = attend(
            queries[:, span].reshape(lines * group, depth),
            keys[:, span].reshape(key_count, depth).astype(bf16),
            values[:, span].reshape(key_count, depth).astype(bf16),
            fixed,
            heads,
        )
        mix[:, span] = gate[:, span] * mixed.reshape(lines, group, depth)
    mixed = mix[...].reshape(rows, depth).astype(bf16)
    result = after[...] + dot(mixed, leave[...])
    hidden = jnp.maximum(dot(normalize(result).astype(bf16), first[...]), 0.0).astype(bf16)
    result = result + dot(hidden, second[...])
    output[...] = result.astype(bf16).reshape(output.shape)


def fetch(sources, buffers, semaphores):
    copies = [
        pltpu.make_async_copy(source, buffer, semaphores.at[index])
        for index, (source, buffer) in enumerate(zip(sources, buffers))
    ]
    for copy in copies:
        copy.start()
    for copy in copies:
        copy.wait()


def split(values):
    high = values.astype(bf16)
    rest = values - high.astype(f32)
    middle = rest.astype(bf16)
    return high, middle, (rest - middle.astype(f32)).astype(bf16)


def store_terms(logit, out, start):
    lanes = out.shape[1]
    parts = [logit[:, first : first + lanes] for first in range(0, logit.shape[1], lanes)]
    values = jnp.concatenate(parts, axis=0)
    held = values.shape[0]
    for index, term in enumerate(split(values)):
        out[start + index * held : start + (index + 1) * held, :] = term


def first_kernel(count, *refs):
    sources, outputs, rest = refs[:count], refs[count : count + 3], refs[count + 3 :]
    buffers, semaphores, tail = rest[:count], rest[count], rest[count + 1]
    fetch(sources, buffers, semaphores)
    embedded, payload, terms = outputs
    embed_kernel(*buffers[:4], embedded, payload, tail)
    pairs, logits = buffers[4:]
    lines, positions, width = pairs.shape
    normed = normalize(pairs[...].astype(f32).reshape(lines * positions, width)).astype(bf16)
    logit = lax.dot_general(logits[...], normed, NT, preferred_element_type=f32)
    store_terms(logit, terms, 0)


def pair_kernel(present, present_row, pairs, entry, gate, near, left):
    lines, positions, width = pairs.shape
    normed = normalize(pairs[...].astype(f32).reshape(lines * positions, width)).astype(bf16)
    projected = dot(normed, entry[...])
    gate[...] = sigmoid(projected[:, 4 * width :])
    left[...] = (sigmoid(projected[:, width : 2 * width]) * projected[:, :width]).astype(bf16)
    operand = sigmoid(projected[:, 3 * width : 4 * width]) * projected[:, 2 * width : 3 * width]
    mask_right(lax.axis_index("res"), operand.astype(bf16), present, present_row, near)


def on_turn():
    return lax.axis_index("res") % 2 == lax.axis_index("aux")


def hold_kernel(terms, present_row, out):
    out[...] = terms[...]


def turn_kernel(pairs, entry, logits, terms, came, given, both):
    lines, positions, width = pairs.shape
    held = terms.shape[0]
    normed = normalize(pairs[...].astype(f32).reshape(lines * positions, width)).astype(bf16)
    projected = dot(normed, entry[:, : 2 * width])
    operand = (sigmoid(projected[:, width:]) * projected[:, :width]).astype(bf16)
    came[...] = operand
    given[...] = operand

    @pl.when(jnp.logical_not(on_turn()))
    def _():
        given[:held, :] = terms[...]

    both[:held, :] = terms[...]
    logit = lax.dot_general(logits[...], normed, NT, preferred_element_type=f32)
    store_terms(logit, both, held)


def gated(pairs, weight):
    lines, positions, width = pairs.shape
    normed = normalize(pairs[...].astype(f32).reshape(lines * positions, width)).astype(bf16)
    projected = dot(normed, weight)
    return (sigmoid(projected[:, width:]) * projected[:, :width]).astype(bf16)


def left_kernel(pairs, entry, left):
    width = pairs.shape[2]
    left[...] = gated(pairs, entry[:, : 2 * width])


def mask_right(source, operand, present, present_row, right):
    lines, positions, width = right.shape
    lane = iota((positions, present_row.shape[1]), 1)
    lane = lane == iota((positions, present_row.shape[1]), 0) + side_index() * positions
    valid = jnp.where(lane, present_row[...].astype(f32), 0.0)
    valid = jnp.sum(valid, axis=1, keepdims=True)
    operand = operand.astype(f32)
    for line in range(lines):
        both = valid * present[source * lines + line].astype(f32)
        right[line] = (operand[line * positions : (line + 1) * positions] * both).astype(
            right.dtype
        )


def right_operand(relative, slot, present, present_row, pairs, entry, right):
    width = pairs.shape[2]
    source = (lax.axis_index("res") ^ slot) if relative else slot
    operand = gated(pairs, entry[:, 2 * width : 4 * width])
    mask_right(source, operand, present, present_row, right)


def pick_left(relative, slot, lefts, left):
    source = (lax.axis_index("res") ^ slot) if relative[0] else slot
    side = side_index()
    for place, block in enumerate(lefts):
        held = (side ^ place) if relative[1] else place

        @pl.when(held == source)
        def _():
            left[...] = block[...].astype(f32).reshape(left.shape)


def accumulate(left, right, total_in, total):
    step = 4
    depth, positions, width = right.shape

    def body(index, carry):
        base = index * step
        sums = [None if total_in is None else total_in[base + t] for t in range(step)]
        for line in range(depth):
            line_right = right[line].astype(f32)
            for t in range(step):
                term = left[line, pl.ds(base + t, 1), :] * line_right
                sums[t] = term if sums[t] is None else sums[t] + term
        for t in range(step):
            total[base + t] = sums[t]
        return carry

    lax.fori_loop(0, total.shape[0] // step, body, 0)


def middle_kernel(relative, slots, *refs):
    rights, lefts = refs[: len(slots)], refs[len(slots) : -2]
    total, left = refs[-2:]
    for index, slot in enumerate(slots):
        pick_left(relative, slot, lefts, left)
        accumulate(left, rights[index], total if index else None, total)


def last_kernel(relative, slot, *refs):
    present, present_row, pairs, entry, total_in, own, gate, leave = refs[:8]
    lefts, (out, left, right, total) = refs[8:-4], refs[-4:]
    lines, positions, width = out.shape
    pick_left(relative, slot, lefts, left)
    right_operand(relative[0], slot, present, present_row, pairs, entry, right)
    accumulate(left, right, total_in, total)
    me = lax.axis_index("res")
    for line in range(lines):
        total[line] = total[line] * present[me * lines + line].astype(f32)
    product = total[...].reshape(lines * positions, width).astype(bf16).astype(f32)
    update = gate[...] * dot(normalize(product).astype(bf16), leave[...])
    out[...] = (own[...].astype(f32) + update.reshape(out.shape)).astype(bf16)


def far_kernel(present, present_row, turned, crossed, entry, right):
    width = turned.shape[2]
    pairs = jnp.where(on_turn(), turned[...].astype(f32), crossed[...].astype(f32))
    operand = gated(pairs, entry[:, 2 * width : 4 * width])
    mask_right(lax.axis_index("res") ^ 1, operand, present, present_row, right)


def accumulate_rows(left, right, total_in, total):
    step = 8

    def body(index, carry):
        base = index * step
        sums = [None if total_in is None else total_in[base + t] for t in range(step)]
        for line in range(right.shape[0]):
            line_right = right[line]
            for t in range(step):
                term = left[line, pl.ds(base + t, 1), :] * line_right
                sums[t] = term if sums[t] is None else sums[t] + term
        for t in range(step):
            total[base + t] = sums[t].astype(total.dtype)
        return carry

    lax.fori_loop(0, total.shape[0] // step, body, 0)


def load_left(block, base, left):
    lines, count, _ = left.shape
    for line in range(lines):
        start = base + line * count
        left[line] = block[start : start + count, :].astype(f32)


def early_kernel(other_half, own, came, other_own, other_came, near, sums, left):
    same = lax.axis_index("br") == lax.axis_index("res") // 2
    mine = jnp.logical_not(same) if other_half else same
    turn = on_turn()
    other, straight = jnp.logical_not(mine), jnp.logical_not(turn)
    pl.when(mine & turn)(lambda: load_left(own, 0, left))
    pl.when(mine & straight)(lambda: load_left(came, 0, left))
    pl.when(other & turn)(lambda: load_left(other_own, 0, left))
    pl.when(other & straight)(lambda: load_left(other_came, 0, left))
    accumulate_rows(left, near, None, sums)


def late_kernel(other_half, came, passed, other_came, other_passed, far, sums, total, left):
    same = lax.axis_index("br") == lax.axis_index("res") // 2
    mine = jnp.logical_not(same) if other_half else same
    turn = on_turn()
    other, straight = jnp.logical_not(mine), jnp.logical_not(turn)
    pl.when(mine & turn)(lambda: load_left(came, 0, left))
    pl.when(mine & straight)(lambda: load_left(passed, 0, left))
    pl.when(other & turn)(lambda: load_left(other_came, 0, left))
    pl.when(other & straight)(lambda: load_left(other_passed, 0, left))
    accumulate_rows(left, far, sums, total)


def finish_kernel(present, kept, own, gate, leave, *refs):
    received, (out, total) = refs[:-2], refs[-2:]
    lines, positions, width = out.shape
    me = lax.axis_index("res")
    each = lines // len(received)
    for line in range(lines):
        sums = kept[line] + received[line // each][line % each].astype(f32)
        total[line] = sums * present[me * lines + line].astype(f32)
    product = total[...].reshape(lines * positions, width).astype(bf16).astype(f32)
    update = gate[...] * dot(normalize(product).astype(bf16), leave[...])
    out[...] = (own[...].astype(f32) + update.reshape(out.shape)).astype(bf16)


def gather(block, axis):
    size = lax.axis_size(axis)
    if size in (1, 2, 4):
        return [block] + [flip(block, axis, d) for d in range(1, size)], True
    whole = lax.all_gather(block, axis)
    return [whole[i] for i in range(size)], False


def flip(block, axis, bit=1):
    return lax.ppermute(block, axis, [(i, i ^ bit) for i in range(lax.axis_size(axis))])


def gather_side(block):
    if lax.axis_size("br") == 2 and lax.axis_size("aux") == 2:
        near = flip(block, "br")
        far = flip(block, "aux")
        return [block, far, near, flip(far, "br")], True
    whole = lax.all_gather(block, SIDE)
    return [whole[i] for i in range(whole.shape[0])], False


def pair_up(block, other, out):
    out[0] = block[...]
    out[1] = other[...]


def double(block, axis, bit, axis_after, ahead):
    far = flip(block, axis, bit)
    pair = call(pair_up, shape((2, *block.shape), block.dtype), after=ahead)(block, far)
    return [pair, flip(pair, axis_after)]


def double_side(block, ahead):
    return double(block, "aux", 1, "br", ahead)


def shape(dims, kind):
    return jax.ShapeDtypeStruct(dims, kind)


def call(kernel, out_shape, scratch=(), smem=0, after=(), hbm=False):
    def run(*args):
        count, unread = len(args), len(after)

        def ordered(*refs):
            kernel(*refs[:count], *refs[count + unread :])

        return pl.pallas_call(
            ordered,
            out_shape=out_shape,
            in_specs=[pl.BlockSpec(memory_space=pltpu.SMEM)] * smem
            + [pl.BlockSpec(memory_space=pltpu.HBM if hbm else pltpu.VMEM)] * (count - smem)
            + [pl.BlockSpec(memory_space=pl.ANY)] * unread,
            out_specs=jax.tree.map(lambda _: pl.BlockSpec(memory_space=pltpu.VMEM), out_shape),
            scratch_shapes=list(scratch),
            compiler_params=pltpu.CompilerParams(vmem_limit_bytes=(62 if hbm else 48) * 1024 * 1024),
            cost_estimate=pl.CostEstimate(flops=1, bytes_accessed=1, transcendentals=0),
        )(*args, *after)

    return run


def triangle_by_gather(pairs, presence, entry, leave, gate):
    res = lax.axis_size("res")
    side = lax.axis_size("br") * lax.axis_size("aux")
    rows, cols, width = pairs.shape
    cube = pltpu.VMEM((rows, cols, width), f32)
    turned = lax.ppermute(
        pairs, ALL, [(r * side + b, b * side + r) for r in range(res) for b in range(side)]
    )
    left = call(left_kernel, shape((rows * cols, width), bf16))(turned, entry)
    lefts, left_relative = gather_side(left)
    blocks, pair_relative = gather(pairs, "res")
    relative = (pair_relative, left_relative)
    slots = list(range(res - 1))
    rights = [
        call(
            functools.partial(right_operand, pair_relative, slot), shape(pairs.shape, bf16), smem=1
        )(*presence, blocks[slot], entry)
        for slot in slots
    ]
    total = call(
        functools.partial(middle_kernel, relative, slots), shape(pairs.shape, f32), [cube]
    )(*rights, *lefts)
    return call(
        functools.partial(last_kernel, relative, res - 1),
        shape(pairs.shape, bf16),
        [cube, cube, cube],
        smem=1,
    )(*presence, blocks[-1], entry, total, pairs, gate, leave, *lefts)


def turn_pairs(pairs):
    index = lambda half, low, br, aux: ((half * 2 + low) * 2 + br) * 2 + aux
    every = [(h, low, br, aux) for h in (0, 1) for low in (0, 1) for br in (0, 1) for aux in (0, 1)]
    goes = lambda h, l, br, a: index(h, l, br, 1 - a) if a == l else index(h, 1 - l, br, a)
    turned = lax.ppermute(pairs, ALL, [(index(*place), goes(*place)) for place in every])
    crossed = lax.ppermute(
        pairs, ALL, [(index(h, l, br, a), index(h, 1 - l, br, a)) for h, l, br, a in every if a == l]
    )
    return turned, crossed


def on_device(
    homolog_features,
    couple_features,
    symbol_ids,
    entry_present,
    amino_present,
    symbol_lookup_matrix,
    horizontal_entry_matrix,
    couple_logit_matrix,
    horizontal_exit_matrix,
    vertical_entry_matrix,
    vertical_exit_matrix,
    feedforward_first_matrix,
    feedforward_second_matrix,
    trimul_entry_matrix,
    trimul_exit_matrix,
):
    lines, positions, depth = homolog_features.shape
    pair_rows, pair_cols, width = couple_features.shape
    heads = couple_logit_matrix.shape[1]
    res = lax.axis_size("res")
    side = lax.axis_size("br") * lax.axis_size("aux")
    rows = lines * positions
    tail = round_up(lines, 16)
    residues = positions * res
    area = pair_rows * pair_cols
    held = pair_rows * pair_cols * heads // width
    presence = [amino_present, amino_present[None, :]]
    halves = (res, lax.axis_size("br"), lax.axis_size("aux")) == (4, 2, 2)

    args = (
        homolog_features,
        symbol_ids,
        entry_present,
        symbol_lookup_matrix,
        couple_features,
        couple_logit_matrix.T,
    )
    embedded, payload, terms = call(
        functools.partial(first_kernel, len(args)),
        (
            shape((rows, depth), f32),
            shape((rows + tail, depth), bf16),
            shape((3 * held, width), bf16),
        ),
        [pltpu.VMEM(x.shape, x.dtype) for x in args]
        + [pltpu.SemaphoreType.DMA((len(args),)), pltpu.VMEM((tail, depth), f32)],
        hbm=True,
    )(*args)
    flat = shape((area, width), bf16)
    of_pairs = lambda pairs: call(
        pair_kernel, (shape((area, width), f32), shape(pairs.shape, f32), flat), smem=1
    )(*presence, pairs, trimul_entry_matrix)
    pending = ()
    if halves:
        row_blocks, row_relative = gather(payload, "res")
        turned, crossed = turn_pairs(couple_features)
        terms = call(hold_kernel, shape(terms.shape, bf16))(terms, presence[1])
        came, given, terms = call(turn_kernel, (flat, flat, shape((6 * held, width), bf16)))(
            turned, trimul_entry_matrix, couple_logit_matrix.T, terms
        )
        passed = flip(given, "aux")
        gate, near, left = of_pairs(lax.optimization_barrier((couple_features, came))[0])
        other_left, other_came = flip(left, "br"), flip(came, "br")
        cube = shape(couple_features.shape, f32)
        scratch = [pltpu.VMEM(couple_features.shape, f32)]
        far = call(far_kernel, cube, smem=1)(*presence, turned, crossed, trimul_entry_matrix)
        ready = lax.optimization_barrier((passed, far, row_blocks[2], row_blocks[3], row_blocks[1]))[0]
        other_passed = flip(ready, "br")
        nearest = lax.optimization_barrier((near, passed, far))[0]
        early = lambda other_half, right: call(
            functools.partial(early_kernel, other_half), cube, scratch
        )(left, came, other_left, other_came, right)
        sent = early(True, nearest)
        operands = (came, passed, other_came, other_passed, far)
        terms, side_relative = (terms, flip(terms, "br"), passed, other_passed), True
        places = [(0, 0, None), (0, 3 * held, 2), (1, 0, None), (1, 3 * held, 3)]
        late = lambda other_half, kind, sums, after: call(
            functools.partial(late_kernel, other_half),
            shape(couple_features.shape, kind),
            scratch,
            after=after,
        )(*operands, sums)
        sent = late(True, bf16, sent, ())
        received = flip(sent, "res", 2)
        pending = (sent,)
    else:
        row_blocks, row_relative = gather(payload, "res")
        gate = of_pairs(couple_features)[0]
        terms, side_relative = gather_side(terms)
        places = [(index, 0, None) for index in range(side)]

    after, payload = call(
        functools.partial(row_kernel, row_relative, side_relative, places, lines, positions),
        (shape((rows, depth), f32), shape((rows + tail, depth), bf16)),
        [
            pltpu.VMEM((pair_rows * heads, residues), f32),
            pltpu.VMEM((lines, residues, depth), bf16),
            pltpu.VMEM((lines, residues, depth), bf16),
            pltpu.VMEM((rows, depth), bf16),
        ],
        after=pending,
    )(*terms, *row_blocks, payload, embedded, horizontal_entry_matrix, horizontal_exit_matrix)
    if halves:
        kept = early(False, lax.optimization_barrier((near, payload))[0])
        column_blocks = double_side(payload, (kept,))
        kept = late(False, f32, kept, ())
        pending = (kept,)
    else:
        column_blocks = gather_side(payload)[0]
    group = 8
    alignment_output = call(
        functools.partial(column_kernel, lines, positions, group, heads),
        shape((lines, positions, depth), bf16),
        [
            pltpu.VMEM((side * lines, positions, depth), f32),
            pltpu.VMEM((side * lines, positions, depth), f32),
            pltpu.VMEM((lines, positions, depth), f32),
        ],
        after=pending,
    )(
        *column_blocks,
        payload,
        after,
        vertical_entry_matrix,
        vertical_exit_matrix,
        feedforward_first_matrix,
        feedforward_second_matrix,
    )
    if halves:
        pair_output = call(
            finish_kernel,
            shape(couple_features.shape, bf16),
            [pltpu.VMEM(couple_features.shape, f32)],
            smem=1,
        )(amino_present, kept, couple_features, gate, trimul_exit_matrix, received)
    else:
        pair_output = triangle_by_gather(
            couple_features, presence, trimul_entry_matrix, trimul_exit_matrix, gate
        )
    return (alignment_output, pair_output)


def solution(mesh):
    return jax.shard_map(
        on_device,
        mesh=mesh,
        in_specs=(
            P(("grp", "br", "aux"), "res", None),
            P(("grp", "res"), ("br", "aux"), None),
            P(("grp", "br", "aux"), "res"),
            P(("grp", "br", "aux"), "res"),
            P("grp"),
            P(),
            P(),
            P(),
            P(),
            P(),
            P(),
            P(),
            P(),
            P(),
            P(),
        ),
        out_specs=(P(("grp", "br", "aux"), "res", None), P(("grp", "res"), ("br", "aux"), None)),
        check_vma=False,
    )
```

```python
import functools

import jax
import jax.numpy as jnp
from jax import lax
from jax.experimental import pallas as pl
from jax.experimental.pallas import tpu as pltpu
from jax.sharding import PartitionSpec as P

epsilon = 1e-05
masked_fill_value = 1000000000.0
bf16 = jnp.bfloat16
f32 = jnp.float32
SIDE = ("br", "aux")
ALL = ("res", "br", "aux")
NT = (((1,), (1,)), ((), ()))
TN = (((0,), (0,)), ((), ()))


def normalize(values):
    average = jnp.mean(values, axis=-1, keepdims=True)
    centred = values - average
    variance = jnp.mean(centred * centred, axis=-1, keepdims=True)
    return centred * lax.rsqrt(variance + epsilon)


def sigmoid(values):
    return 1.0 / (1.0 + jnp.exp(-values))


def dot(left, right):
    return jnp.dot(left, right, preferred_element_type=f32)


def iota(shape, dim):
    return lax.broadcasted_iota(jnp.int32, shape, dim)


def round_up(count, step):
    return -(-count // step) * step


def side_index():
    return lax.axis_index("br") * lax.axis_size("aux") + lax.axis_index("aux")


def embed_kernel(features, ids, present, table, embedded, payload, tail):
    lines, positions, depth = features.shape
    kinds = table.shape[0]
    rows = lines * positions
    for line in range(lines):
        onehot = (iota((kinds, positions), 0) == ids[line : line + 1, :]).astype(bf16)
        token = lax.dot_general(onehot, table[...], TN, preferred_element_type=f32)
        values = features[line].astype(f32) + token
        span = slice(line * positions, (line + 1) * positions)
        embedded[span, :] = values
        payload[span, :] = normalize(values).astype(bf16)
    tail[...] = jnp.zeros_like(tail)
    tail[:lines, :positions] = present[...].astype(f32)
    payload[rows:, :] = tail[...].astype(bf16)


def attend(queries, keys, values, bias, heads):
    count, depth = queries.shape
    width = depth // heads
    own = (iota((heads, depth), 1) // width == iota((heads, depth), 0)).astype(f32)
    spread = (queries[:, None, :] * own[None]).reshape(count * heads, depth).astype(bf16)
    scores = lax.dot_general(spread, keys, NT, preferred_element_type=f32) * width ** (-0.5)
    scores = bias(scores)
    powers = jnp.exp(scores - jnp.max(scores, axis=-1, keepdims=True))
    weights = (powers * (1.0 / jnp.sum(powers, axis=-1, keepdims=True))).astype(bf16)
    mixed = dot(weights, values).reshape(count, heads, depth)
    return jnp.sum(mixed * own[None], axis=1)


def row_kernel(relative, side_relative, places, lines, positions, *refs):
    used = 1 + max(max(index, index if other is None else other) for index, _, other in places)
    terms, refs = refs[:used], refs[used:]
    blocks = refs[: len(refs) - 10]
    own, embedded, entry, leave, after, payload, bias, keys, values, mix = refs[len(refs) - 10 :]
    depth = leave.shape[0]
    heads = bias.shape[0] // positions
    rows = lines * positions
    key_count = bias.shape[1]
    me = lax.axis_index("res")
    lanes = terms[0].shape[1]
    per = lanes // positions
    side = side_index()
    sums = []
    held = positions * heads // per
    sums = []
    for source, start, other in places:
        parts = []
        for index in range(3):
            first = index * held
            part = terms[source][start + first : start + first + held, :].astype(f32)
            if other is not None:
                choice = terms[other][first : first + held, :].astype(f32)
                part = jnp.where(on_turn(), choice, part)
            parts.append(part)
        sums.append(parts[0] + parts[1] + parts[2])
    place = iota((heads, key_count), 1) // positions
    for line in range(positions):
        total = jnp.zeros((heads, key_count), f32)
        for slot, values_of in enumerate(sums):
            source = (side ^ slot) if side_relative else slot
            part = values_of[(line // per) * heads : (line // per + 1) * heads]
            part = pltpu.roll(part, ((source - line % per + lanes) % per) * positions, 1)
            part = jnp.concatenate([part] * (key_count // lanes), axis=1)
            total = jnp.where(place == source, part, total)
        bias[line * heads : (line + 1) * heads, :] = total
    penalty = jnp.zeros((payload.shape[0] - rows, key_count), f32)
    for slot, block in enumerate(blocks):
        source = (me ^ slot) if relative else slot
        place = iota((depth, key_count), 0)
        place = (place < positions) & (iota((depth, key_count), 1) == place + source * positions)
        penalty += dot(block[rows:, :], place.astype(bf16))
        projected = dot(block[:rows, :], entry[:, depth : 3 * depth]).astype(bf16)
        for line in range(lines):
            span = pl.ds(pl.multiple_of(source * positions, positions), positions)
            part = projected[line * positions : (line + 1) * positions]
            keys[line, span, :] = part[:, :depth]
            values[line, span, :] = part[:, depth:]
    penalty = masked_fill_value * (penalty - 1.0)
    normed = own[:rows, :]
    queries = dot(normed, entry[:, :depth]).astype(bf16).astype(f32)
    gate = sigmoid(dot(normed, entry[:, 3 * depth :]))
    for line in range(lines):
        span = slice(line * positions, (line + 1) * positions)
        fixed = lambda scores, line=line: scores + bias[...] + penalty[line : line + 1, :]
        mixed = attend(queries[span], keys[line], values[line], fixed, heads)
        mix[span, :] = (gate[span] * mixed).astype(bf16)
    result = embedded[...] + dot(mix[...], leave[...])
    after[...] = result
    payload[:rows, :] = normalize(result).astype(bf16)
    payload[rows:, :] = own[rows:, :]


def column_kernel(lines, positions, group, heads, *refs):
    blocks = refs[: len(refs) - 10]
    own, after, entry, leave, first, second, output, keys, values, mix = refs[len(refs) - 10 :]
    depth = leave.shape[0]
    rows = lines * positions
    presence = []
    blocks = [
        block.at[part] if len(block.shape) == 3 else block
        for block in blocks
        for part in range(block.shape[0] if len(block.shape) == 3 else 1)
    ]
    for slot, block in enumerate(blocks):
        projected = dot(block[:rows, :], entry[:, depth : 3 * depth])
        span = slice(slot * lines, (slot + 1) * lines)
        keys[span] = projected[:, :depth].reshape(lines, positions, depth)
        values[span] = projected[:, depth:].reshape(lines, positions, depth)
        presence.append(block[rows:, :])
    tail = presence[0].shape[0]
    presence = jnp.concatenate(presence, axis=0)
    normed = own[:rows, :]
    queries = dot(normed, entry[:, :depth]).astype(bf16).astype(f32)
    queries = queries.reshape(lines, positions, depth)
    gate = sigmoid(dot(normed, entry[:, 3 * depth :])).reshape(lines, positions, depth)
    key_count = len(blocks) * lines * group
    row = iota((presence.shape[0], key_count), 0)
    lane = iota((presence.shape[0], key_count), 1)
    chosen = (row % tail < lines) & ((row // tail) * lines + row % tail == lane // group)
    shape = (lines * group * heads, key_count)
    same = (iota(shape, 0) // heads) % group == iota(shape, 1) % group
    for start in range(0, positions, group):
        span = slice(start, start + group)
        pick = (iota((depth, key_count), 0) == start + iota((depth, key_count), 1) % group)
        held = dot(presence, pick.astype(bf16))
        held = jnp.sum(jnp.where(chosen, held, 0.0), axis=0, keepdims=True)
        penalty = masked_fill_value * (held - 1.0)
        fixed = lambda scores: jnp.where(same, scores + penalty, -jnp.inf)
        mixed = attend(
            queries[:, span].reshape(lines * group, depth),
            keys[:, span].reshape(key_count, depth).astype(bf16),
            values[:, span].reshape(key_count, depth).astype(bf16),
            fixed,
            heads,
        )
        mix[:, span] = gate[:, span] * mixed.reshape(lines, group, depth)
    mixed = mix[...].reshape(rows, depth).astype(bf16)
    result = after[...] + dot(mixed, leave[...])
    hidden = jnp.maximum(dot(normalize(result).astype(bf16), first[...]), 0.0).astype(bf16)
    result = result + dot(hidden, second[...])
    output[...] = result.astype(bf16).reshape(output.shape)


def fetch(sources, buffers, semaphores):
    copies = [
        pltpu.make_async_copy(source, buffer, semaphores.at[index])
        for index, (source, buffer) in enumerate(zip(sources, buffers))
    ]
    for copy in copies:
        copy.start()
    for copy in copies:
        copy.wait()


def split(values):
    high = values.astype(bf16)
    rest = values - high.astype(f32)
    middle = rest.astype(bf16)
    return high, middle, (rest - middle.astype(f32)).astype(bf16)


def store_terms(logit, out, start):
    lanes = out.shape[1]
    parts = [logit[:, first : first + lanes] for first in range(0, logit.shape[1], lanes)]
    values = jnp.concatenate(parts, axis=0)
    held = values.shape[0]
    for index, term in enumerate(split(values)):
        out[start + index * held : start + (index + 1) * held, :] = term


def first_kernel(count, *refs):
    sources, outputs, rest = refs[:count], refs[count : count + 3], refs[count + 3 :]
    buffers, semaphores, tail = rest[:count], rest[count], rest[count + 1]
    fetch(sources, buffers, semaphores)
    embedded, payload, terms = outputs
    embed_kernel(*buffers[:4], embedded, payload, tail)
    pairs, logits = buffers[4:]
    lines, positions, width = pairs.shape
    normed = normalize(pairs[...].astype(f32).reshape(lines * positions, width)).astype(bf16)
    logit = lax.dot_general(logits[...], normed, NT, preferred_element_type=f32)
    store_terms(logit, terms, 0)


def pair_kernel(present, present_row, pairs, entry, gate, near, left):
    lines, positions, width = pairs.shape
    normed = normalize(pairs[...].astype(f32).reshape(lines * positions, width)).astype(bf16)
    projected = dot(normed, entry[...])
    gate[...] = sigmoid(projected[:, 4 * width :])
    left[...] = (sigmoid(projected[:, width : 2 * width]) * projected[:, :width]).astype(bf16)
    operand = sigmoid(projected[:, 3 * width : 4 * width]) * projected[:, 2 * width : 3 * width]
    mask_right(lax.axis_index("res"), operand.astype(bf16), present, present_row, near)


def on_turn():
    return lax.axis_index("res") % 2 == lax.axis_index("aux")


def hold_kernel(terms, present_row, out):
    out[...] = terms[...]


def turn_kernel(pairs, entry, logits, terms, came, given, both):
    lines, positions, width = pairs.shape
    held = terms.shape[0]
    normed = normalize(pairs[...].astype(f32).reshape(lines * positions, width)).astype(bf16)
    projected = dot(normed, entry[:, : 2 * width])
    operand = (sigmoid(projected[:, width:]) * projected[:, :width]).astype(bf16)
    came[...] = operand
    given[...] = operand

    @pl.when(jnp.logical_not(on_turn()))
    def _():
        given[:held, :] = terms[...]

    both[:held, :] = terms[...]
    logit = lax.dot_general(logits[...], normed, NT, preferred_element_type=f32)
    store_terms(logit, both, held)


def gated(pairs, weight):
    lines, positions, width = pairs.shape
    normed = normalize(pairs[...].astype(f32).reshape(lines * positions, width)).astype(bf16)
    projected = dot(normed, weight)
    return (sigmoid(projected[:, width:]) * projected[:, :width]).astype(bf16)


def left_kernel(pairs, entry, left):
    width = pairs.shape[2]
    left[...] = gated(pairs, entry[:, : 2 * width])


def mask_right(source, operand, present, present_row, right):
    lines, positions, width = right.shape
    lane = iota((positions, present_row.shape[1]), 1)
    lane = lane == iota((positions, present_row.shape[1]), 0) + side_index() * positions
    valid = jnp.where(lane, present_row[...].astype(f32), 0.0)
    valid = jnp.sum(valid, axis=1, keepdims=True)
    operand = operand.astype(f32)
    for line in range(lines):
        both = valid * present[source * lines + line].astype(f32)
        right[line] = (operand[line * positions : (line + 1) * positions] * both).astype(
            right.dtype
        )


def right_operand(relative, slot, present, present_row, pairs, entry, right):
    width = pairs.shape[2]
    source = (lax.axis_index("res") ^ slot) if relative else slot
    operand = gated(pairs, entry[:, 2 * width : 4 * width])
    mask_right(source, operand, present, present_row, right)


def pick_left(relative, slot, lefts, left):
    source = (lax.axis_index("res") ^ slot) if relative[0] else slot
    side = side_index()
    for place, block in enumerate(lefts):
        held = (side ^ place) if relative[1] else place

        @pl.when(held == source)
        def _():
            left[...] = block[...].astype(f32).reshape(left.shape)


def accumulate(left, right, total_in, total):
    step = 4
    depth, positions, width = right.shape

    def body(index, carry):
        base = index * step
        sums = [None if total_in is None else total_in[base + t] for t in range(step)]
        for line in range(depth):
            line_right = right[line].astype(f32)
            for t in range(step):
                term = left[line, pl.ds(base + t, 1), :] * line_right
                sums[t] = term if sums[t] is None else sums[t] + term
        for t in range(step):
            total[base + t] = sums[t]
        return carry

    lax.fori_loop(0, total.shape[0] // step, body, 0)


def middle_kernel(relative, slots, *refs):
    rights, lefts = refs[: len(slots)], refs[len(slots) : -2]
    total, left = refs[-2:]
    for index, slot in enumerate(slots):
        pick_left(relative, slot, lefts, left)
        accumulate(left, rights[index], total if index else None, total)


def last_kernel(relative, slot, *refs):
    present, present_row, pairs, entry, total_in, own, gate, leave = refs[:8]
    lefts, (out, left, right, total) = refs[8:-4], refs[-4:]
    lines, positions, width = out.shape
    pick_left(relative, slot, lefts, left)
    right_operand(relative[0], slot, present, present_row, pairs, entry, right)
    accumulate(left, right, total_in, total)
    me = lax.axis_index("res")
    for line in range(lines):
        total[line] = total[line] * present[me * lines + line].astype(f32)
    product = total[...].reshape(lines * positions, width).astype(bf16).astype(f32)
    update = gate[...] * dot(normalize(product).astype(bf16), leave[...])
    out[...] = (own[...].astype(f32) + update.reshape(out.shape)).astype(bf16)


def far_kernel(present, present_row, turned, crossed, entry, right):
    width = turned.shape[2]
    pairs = jnp.where(on_turn(), turned[...].astype(f32), crossed[...].astype(f32))
    operand = gated(pairs, entry[:, 2 * width : 4 * width])
    mask_right(lax.axis_index("res") ^ 1, operand, present, present_row, right)


def accumulate_rows(left, right, total_in, total):
    step = 8

    def body(index, carry):
        base = index * step
        sums = [None if total_in is None else total_in[base + t] for t in range(step)]
        for line in range(right.shape[0]):
            line_right = right[line]
            for t in range(step):
                term = left[line, pl.ds(base + t, 1), :] * line_right
                sums[t] = term if sums[t] is None else sums[t] + term
        for t in range(step):
            total[base + t] = sums[t].astype(total.dtype)
        return carry

    lax.fori_loop(0, total.shape[0] // step, body, 0)


def load_left(block, base, left):
    lines, count, _ = left.shape
    for line in range(lines):
        start = base + line * count
        left[line] = block[start : start + count, :].astype(f32)


def early_kernel(other_half, own, came, other_own, other_came, near, sums, left):
    same = lax.axis_index("br") == lax.axis_index("res") // 2
    mine = jnp.logical_not(same) if other_half else same
    turn = on_turn()
    other, straight = jnp.logical_not(mine), jnp.logical_not(turn)
    pl.when(mine & turn)(lambda: load_left(own, 0, left))
    pl.when(mine & straight)(lambda: load_left(came, 0, left))
    pl.when(other & turn)(lambda: load_left(other_own, 0, left))
    pl.when(other & straight)(lambda: load_left(other_came, 0, left))
    accumulate_rows(left, near, None, sums)


def late_kernel(other_half, came, passed, other_came, other_passed, far, sums, total, left):
    same = lax.axis_index("br") == lax.axis_index("res") // 2
    mine = jnp.logical_not(same) if other_half else same
    turn = on_turn()
    other, straight = jnp.logical_not(mine), jnp.logical_not(turn)
    pl.when(mine & turn)(lambda: load_left(came, 0, left))
    pl.when(mine & straight)(lambda: load_left(passed, 0, left))
    pl.when(other & turn)(lambda: load_left(other_came, 0, left))
    pl.when(other & straight)(lambda: load_left(other_passed, 0, left))
    accumulate_rows(left, far, sums, total)


def finish_kernel(present, kept, own, gate, leave, *refs):
    received, (out, total) = refs[:-2], refs[-2:]
    lines, positions, width = out.shape
    me = lax.axis_index("res")
    each = lines // len(received)
    for line in range(lines):
        sums = kept[line] + received[line // each][line % each].astype(f32)
        total[line] = sums * present[me * lines + line].astype(f32)
    product = total[...].reshape(lines * positions, width).astype(bf16).astype(f32)
    update = gate[...] * dot(normalize(product).astype(bf16), leave[...])
    out[...] = (own[...].astype(f32) + update.reshape(out.shape)).astype(bf16)


def gather(block, axis):
    size = lax.axis_size(axis)
    if size in (1, 2, 4):
        return [block] + [flip(block, axis, d) for d in range(1, size)], True
    whole = lax.all_gather(block, axis)
    return [whole[i] for i in range(size)], False


def flip(block, axis, bit=1):
    return lax.ppermute(block, axis, [(i, i ^ bit) for i in range(lax.axis_size(axis))])


def gather_side(block):
    if lax.axis_size("br") == 2 and lax.axis_size("aux") == 2:
        near = flip(block, "br")
        far = flip(block, "aux")
        return [block, far, near, flip(far, "br")], True
    whole = lax.all_gather(block, SIDE)
    return [whole[i] for i in range(whole.shape[0])], False


def pair_up(block, other, out):
    out[0] = block[...]
    out[1] = other[...]


def double(block, axis, bit, axis_after, ahead):
    far = flip(block, axis, bit)
    pair = call(pair_up, shape((2, *block.shape), block.dtype), after=ahead)(block, far)
    return [pair, flip(pair, axis_after)]


def double_side(block, ahead):
    return double(block, "aux", 1, "br", ahead)


def shape(dims, kind):
    return jax.ShapeDtypeStruct(dims, kind)


def call(kernel, out_shape, scratch=(), smem=0, after=(), hbm=False):
    def run(*args):
        count, unread = len(args), len(after)

        def ordered(*refs):
            kernel(*refs[:count], *refs[count + unread :])

        return pl.pallas_call(
            ordered,
            out_shape=out_shape,
            in_specs=[pl.BlockSpec(memory_space=pltpu.SMEM)] * smem
            + [pl.BlockSpec(memory_space=pltpu.HBM if hbm else pltpu.VMEM)] * (count - smem)
            + [pl.BlockSpec(memory_space=pl.ANY)] * unread,
            out_specs=jax.tree.map(lambda _: pl.BlockSpec(memory_space=pltpu.VMEM), out_shape),
            scratch_shapes=list(scratch),
            compiler_params=pltpu.CompilerParams(vmem_limit_bytes=(62 if hbm else 48) * 1024 * 1024),
            cost_estimate=pl.CostEstimate(flops=1, bytes_accessed=1, transcendentals=0),
        )(*args, *after)

    return run


def triangle_by_gather(pairs, presence, entry, leave, gate):
    res = lax.axis_size("res")
    side = lax.axis_size("br") * lax.axis_size("aux")
    rows, cols, width = pairs.shape
    cube = pltpu.VMEM((rows, cols, width), f32)
    turned = lax.ppermute(
        pairs, ALL, [(r * side + b, b * side + r) for r in range(res) for b in range(side)]
    )
    left = call(left_kernel, shape((rows * cols, width), bf16))(turned, entry)
    lefts, left_relative = gather_side(left)
    blocks, pair_relative = gather(pairs, "res")
    relative = (pair_relative, left_relative)
    slots = list(range(res - 1))
    rights = [
        call(
            functools.partial(right_operand, pair_relative, slot), shape(pairs.shape, bf16), smem=1
        )(*presence, blocks[slot], entry)
        for slot in slots
    ]
    total = call(
        functools.partial(middle_kernel, relative, slots), shape(pairs.shape, f32), [cube]
    )(*rights, *lefts)
    return call(
        functools.partial(last_kernel, relative, res - 1),
        shape(pairs.shape, bf16),
        [cube, cube, cube],
        smem=1,
    )(*presence, blocks[-1], entry, total, pairs, gate, leave, *lefts)


def turn_pairs(pairs):
    index = lambda half, low, br, aux: ((half * 2 + low) * 2 + br) * 2 + aux
    every = [(h, low, br, aux) for h in (0, 1) for low in (0, 1) for br in (0, 1) for aux in (0, 1)]
    goes = lambda h, l, br, a: index(h, l, br, 1 - a) if a == l else index(h, 1 - l, br, a)
    turned = lax.ppermute(pairs, ALL, [(index(*place), goes(*place)) for place in every])
    crossed = lax.ppermute(
        pairs, ALL, [(index(h, l, br, a), index(h, 1 - l, br, a)) for h, l, br, a in every if a == l]
    )
    return turned, crossed


def on_device(
    homolog_features,
    couple_features,
    symbol_ids,
    entry_present,
    amino_present,
    symbol_lookup_matrix,
    horizontal_entry_matrix,
    couple_logit_matrix,
    horizontal_exit_matrix,
    vertical_entry_matrix,
    vertical_exit_matrix,
    feedforward_first_matrix,
    feedforward_second_matrix,
    trimul_entry_matrix,
    trimul_exit_matrix,
):
    lines, positions, depth = homolog_features.shape
    pair_rows, pair_cols, width = couple_features.shape
    heads = couple_logit_matrix.shape[1]
    res = lax.axis_size("res")
    side = lax.axis_size("br") * lax.axis_size("aux")
    rows = lines * positions
    tail = round_up(lines, 16)
    residues = positions * res
    area = pair_rows * pair_cols
    held = pair_rows * pair_cols * heads // width
    presence = [amino_present, amino_present[None, :]]
    halves = (res, lax.axis_size("br"), lax.axis_size("aux")) == (4, 2, 2)

    args = (
        homolog_features,
        symbol_ids,
        entry_present,
        symbol_lookup_matrix,
        couple_features,
        couple_logit_matrix.T,
    )
    embedded, payload, terms = call(
        functools.partial(first_kernel, len(args)),
        (
            shape((rows, depth), f32),
            shape((rows + tail, depth), bf16),
            shape((3 * held, width), bf16),
        ),
        [pltpu.VMEM(x.shape, x.dtype) for x in args]
        + [pltpu.SemaphoreType.DMA((len(args),)), pltpu.VMEM((tail, depth), f32)],
        hbm=True,
    )(*args)
    flat = shape((area, width), bf16)
    of_pairs = lambda pairs: call(
        pair_kernel, (shape((area, width), f32), shape(pairs.shape, f32), flat), smem=1
    )(*presence, pairs, trimul_entry_matrix)
    pending = ()
    if halves:
        row_blocks, row_relative = gather(payload, "res")
        turned, crossed = turn_pairs(couple_features)
        terms = call(hold_kernel, shape(terms.shape, bf16))(terms, presence[1])
        came, given, terms = call(turn_kernel, (flat, flat, shape((6 * held, width), bf16)))(
            turned, trimul_entry_matrix, couple_logit_matrix.T, terms
        )
        passed = flip(given, "aux")
        gate, near, left = of_pairs(lax.optimization_barrier((couple_features, came))[0])
        other_left, other_came = flip(left, "br"), flip(came, "br")
        cube = shape(couple_features.shape, f32)
        scratch = [pltpu.VMEM(couple_features.shape, f32)]
        far = call(far_kernel, cube, smem=1)(*presence, turned, crossed, trimul_entry_matrix)
        ready = lax.optimization_barrier((passed, row_blocks[2], row_blocks[3], row_blocks[1]))[0]
        other_passed = flip(ready, "br")
        nearest = lax.optimization_barrier((near, passed, far))[0]
        early = lambda other_half, right: call(
            functools.partial(early_kernel, other_half), cube, scratch
        )(left, came, other_left, other_came, right)
        sent = early(True, nearest)
        operands = (came, passed, other_came, other_passed, far)
        terms, side_relative = (terms, flip(terms, "br"), passed, other_passed), True
        places = [(0, 0, None), (0, 3 * held, 2), (1, 0, None), (1, 3 * held, 3)]
        late = lambda other_half, kind, sums, after: call(
            functools.partial(late_kernel, other_half),
            shape(couple_features.shape, kind),
            scratch,
            after=after,
        )(*operands, sums)
        sent = late(True, bf16, sent, ())
        received = flip(sent, "res", 2)
        pending = (sent,)
    else:
        row_blocks, row_relative = gather(payload, "res")
        gate = of_pairs(couple_features)[0]
        terms, side_relative = gather_side(terms)
        places = [(index, 0, None) for index in range(side)]

    after, payload = call(
        functools.partial(row_kernel, row_relative, side_relative, places, lines, positions),
        (shape((rows, depth), f32), shape((rows + tail, depth), bf16)),
        [
            pltpu.VMEM((pair_rows * heads, residues), f32),
            pltpu.VMEM((lines, residues, depth), bf16),
            pltpu.VMEM((lines, residues, depth), bf16),
            pltpu.VMEM((rows, depth), bf16),
        ],
        after=pending,
    )(*terms, *row_blocks, payload, embedded, horizontal_entry_matrix, horizontal_exit_matrix)
    if halves:
        kept = early(False, lax.optimization_barrier((near, payload))[0])
        column_blocks = double_side(payload, (kept,))
        kept = late(False, f32, kept, ())
        pending = (kept,)
    else:
        column_blocks = gather_side(payload)[0]
    group = 8
    alignment_output = call(
        functools.partial(column_kernel, lines, positions, group, heads),
        shape((lines, positions, depth), bf16),
        [
            pltpu.VMEM((side * lines, positions, depth), f32),
            pltpu.VMEM((side * lines, positions, depth), f32),
            pltpu.VMEM((lines, positions, depth), f32),
        ],
        after=pending,
    )(
        *column_blocks,
        payload,
        after,
        vertical_entry_matrix,
        vertical_exit_matrix,
        feedforward_first_matrix,
        feedforward_second_matrix,
    )
    if halves:
        pair_output = call(
            finish_kernel,
            shape(couple_features.shape, bf16),
            [pltpu.VMEM(couple_features.shape, f32)],
            smem=1,
        )(amino_present, kept, couple_features, gate, trimul_exit_matrix, received)
    else:
        pair_output = triangle_by_gather(
            couple_features, presence, trimul_entry_matrix, trimul_exit_matrix, gate
        )
    return (alignment_output, pair_output)


def solution(mesh):
    return jax.shard_map(
        on_device,
        mesh=mesh,
        in_specs=(
            P(("grp", "br", "aux"), "res", None),
            P(("grp", "res"), ("br", "aux"), None),
            P(("grp", "br", "aux"), "res"),
            P(("grp", "br", "aux"), "res"),
            P("grp"),
            P(),
            P(),
            P(),
            P(),
            P(),
            P(),
            P(),
            P(),
            P(),
            P(),
        ),
        out_specs=(P(("grp", "br", "aux"), "res", None), P(("grp", "res"), ("br", "aux"), None)),
        check_vma=False,
    )
```
